128 devices in a mesh: row: 16 (over z, y_lo, core), col: 8 (over x, y_hi).
Axes of the slice: x: 4, y: 4 (y_hi: 2, y_lo: 2; y = y_hi * 2 + y_lo), z: 4, core: 2. Of those that a mesh axis runs over, the one named last changes fastest.
Arguments:
- pair: bfloat16 [512, 512, 128], P('row', 'col'), may hold values from -6 to 6
- residue_mask: int32 [512], replicated, may hold values 0 or 1
- out_in_w: bfloat16 [128, 512], replicated, may hold values from -0.5 to 0.5
- out_gate_w: bfloat16 [128, 128], replicated, may hold values from -0.5 to 0.5
- out_out_w: bfloat16 [128, 128], replicated, may hold values from -0.5 to 0.5
- inc_in_w: bfloat16 [128, 512], replicated, may hold values from -0.5 to 0.5
- inc_gate_w: bfloat16 [128, 128], replicated, may hold values from -0.5 to 0.5
- inc_out_w: bfloat16 [128, 128], replicated, may hold values from -0.5 to 0.5
- trans_up: bfloat16 [128, 1024], replicated, may hold values from -0.5 to 0.5
- trans_down: bfloat16 [512, 128], replicated, may hold values from -0.25 to 0.25
Outputs:
- updated: bfloat16 [512, 512, 128], P('row', 'col')
The draws below stay inside these ranges and needn't reach their ends.
All inputs are finite; a program needn't handle non-finite values.
Results may differ from the reference program's by a relative error of at most 0.014.
Values may be sent and summed in bfloat16 or wider, within the bound.
No kernel may reach another device: no remote copies, remote signals or barrier semaphores. Data moves between devices by JAX's collectives and lax.ppermute only.
A program may use at most 128 MiB of HBM per device.

```python
import jax
import jax.numpy as jnp
from jax import lax

C = 128
H = 128
TRANS = 512
N = 512


def with_ends(result, stream_key, smallest, top_value):
    longest = result.shape.index(max(result.shape))
    spots = []
    for shift in (0, 1):
        where = [jax.random.randint(jax.random.fold_in(stream_key, axis), (), 0, length) for axis, length in enumerate(result.shape)]
        where[longest] = (where[longest] + shift) % result.shape[longest]
        spots.append(tuple(where))
    return result.at[spots[0]].set(smallest).at[spots[1]].set(top_value)


def shard_levels(stream_key, dims, shards, least, top_value):
    def one(axis_at, blocks):
        steps = jax.random.uniform(jax.random.fold_in(jax.random.fold_in(stream_key, 6), axis_at), (blocks,), jnp.float32, least / len(shards), top_value / len(shards))
        return jnp.repeat(jnp.exp(steps), dims[axis_at] // blocks).reshape((-1,) + (1,) * (len(dims) - axis_at - 1))

    level = one(*shards[0])
    for cut in shards[1:]:
        level = level * one(*cut)
    return level


def noise(key, extent, scale, reach, pieces=(), kind=jnp.bfloat16):
    result = jax.random.normal(key, extent, jnp.float32) * scale
    if len(pieces) > 0:
        result = shard_levels(key, extent, pieces, -0.22, 0.18) * result
    return jnp.clip(result, min=-reach, max=reach).astype(kind)


def setup_inputs(seed: int = 0) -> dict:
    streams_of = jax.random.split(jax.random.key(seed), 11)
    return {
        "pair": noise(streams_of[0], (N, N, C), 1.0, 6.0, ((0, 16), (1, 8))),
        "residue_mask": with_ends((jax.random.randint(streams_of[1], (N,), 0, 8) < 7).astype(jnp.int32), jax.random.fold_in(streams_of[1], 1), 0, 1),
        "out_in_w": noise(streams_of[2], (C, 4 * H), C ** -0.5, 0.5),
        "out_gate_w": noise(streams_of[3], (C, C), C ** -0.5, 0.5),
        "out_out_w": noise(streams_of[4], (H, C), H ** -0.5, 0.5),
        "inc_in_w": noise(streams_of[5], (C, 4 * H), C ** -0.5, 0.5),
        "inc_gate_w": noise(streams_of[6], (C, C), C ** -0.5, 0.5),
        "inc_out_w": noise(streams_of[7], (H, C), H ** -0.5, 0.5),
        "trans_up": noise(streams_of[8], (C, 2 * TRANS), C ** -0.5, 0.5),
        "trans_down": noise(streams_of[9], (TRANS, C), TRANS ** -0.5, 0.25),
    }


def layer_norm(values):
    center = values - lax.optimization_barrier(jnp.mean(values, axis=-1, keepdims=True))
    spread = lax.optimization_barrier(jnp.mean(center * center, axis=-1, keepdims=True))
    return center * lax.rsqrt(spread + 1e-05)

def triangle_update(pair, residue_mask, w_in, w_gate, w_out, incoming):
    pair_f = pair.astype(jnp.float32)
    normed = layer_norm(pair_f).astype(jnp.bfloat16)
    flat = normed.reshape(N * N, C)
    projected = jnp.dot(flat, w_in, preferred_element_type=jnp.float32).reshape(N, N, 4 * H)
    present = residue_mask.astype(jnp.float32)
    weight_mask = (present[:, None] * present[None, :])[:, :, None]
    left = (weight_mask * jax.nn.sigmoid(projected[..., 0:H]) * projected[..., H:2 * H]).astype(jnp.bfloat16)
    right = (weight_mask * jax.nn.sigmoid(projected[..., 2 * H:3 * H]) * projected[..., 3 * H:4 * H]).astype(jnp.bfloat16)
    left_f = jnp.transpose(left, (2, 0, 1)).astype(jnp.float32)
    right_f = jnp.transpose(right, (2, 0, 1)).astype(jnp.float32)
    if incoming:
        mixed = jnp.einsum('hki,hkj->hij', left_f, right_f)
    else:
        mixed = jnp.einsum('hik,hjk->hij', left_f, right_f)
    centered = mixed - lax.optimization_barrier(jnp.mean(mixed, axis=0, keepdims=True))
    spread = lax.optimization_barrier(jnp.mean(centered * centered, axis=0, keepdims=True))
    scaled = (centered * lax.rsqrt(jnp.maximum(spread, 1.0))).astype(jnp.bfloat16)
    gate = jax.nn.sigmoid(jnp.dot(flat, w_gate, preferred_element_type=jnp.float32)).reshape(N, N, C)
    update = jnp.einsum('hij,hc->ijc', scaled.astype(jnp.float32), w_out.astype(jnp.float32))
    return (pair_f + gate * update).astype(jnp.bfloat16)

def reference(pair, residue_mask, out_in_w, out_gate_w, out_out_w, inc_in_w, inc_gate_w, inc_out_w, trans_up, trans_down):
    first = triangle_update(pair, residue_mask, out_in_w, out_gate_w, out_out_w, False)
    second = triangle_update(first, residue_mask, inc_in_w, inc_gate_w, inc_out_w, True)
    second_f = second.astype(jnp.float32)
    normed = layer_norm(second_f).astype(jnp.bfloat16).reshape(N * N, C)
    raised = jnp.dot(normed, trans_up, preferred_element_type=jnp.float32)
    hidden = (jax.nn.silu(raised[:, 0:TRANS]) * raised[:, TRANS:2 * TRANS]).astype(jnp.bfloat16)
    lowered = jnp.dot(hidden, trans_down, preferred_element_type=jnp.float32).reshape(N, N, C)
    return (second_f + lowered).astype(jnp.bfloat16)
```

```python
import functools

import jax
import jax.numpy as jnp
from jax import lax
from jax.experimental import pallas as pl
from jax.experimental.pallas import tpu as pltpu
from jax.sharding import PartitionSpec as P

F32 = jnp.float32
BF16 = jnp.bfloat16
ROWS, COLS, CHANS = 32, 64, 128
HALF = ROWS // 2
LANES = 2 * COLS
DEVS = 128


def sigmoid(x):
    return 0.5 * jnp.tanh(0.5 * x) + 0.5


def normalize(x):
    center = x - jnp.mean(x, axis=0, keepdims=True)
    spread = jnp.mean(center * center, axis=0, keepdims=True)
    return (center * lax.rsqrt(spread + 1e-05)).astype(BF16)


def tile_mask(rows_ref, cols_ref):
    row0 = lax.axis_index("row") * ROWS
    col = lax.axis_index("col")
    line = cols_ref[pl.ds(col // 2, 1), :].astype(F32)
    swapped = pltpu.roll(line, COLS, 1)
    lane = lax.broadcasted_iota(jnp.int32, (1, LANES), 1)
    low = lane < COLS
    even = (col % 2) == 0
    cols = jnp.where(low == even, line, swapped)

    def at(s):
        top = rows_ref[row0 + s].astype(F32)
        bottom = rows_ref[row0 + HALF + s].astype(F32)
        return cols * jnp.where(low, top, bottom)

    return at


def project(x, w, mask_at, s0, count, stage):
    normed = normalize(x)
    p = jnp.dot(w, normed, preferred_element_type=F32)
    mask = jnp.concatenate([mask_at(s0 + n) for n in range(count)], axis=1)
    left = mask * sigmoid(p[0:128]) * p[128:256]
    right = mask * sigmoid(p[256:384]) * p[384:512]
    for n in range(count):
        lanes = slice(n * LANES, (n + 1) * LANES)
        stage[pl.ds(s0 + n, 128, stride=2 * HALF), :] = left[:, lanes]
        stage[pl.ds(HALF + s0 + n, 128, stride=2 * HALF), :] = right[:, lanes]
    return sigmoid(p[512:640])


def put_pieces(stage, pieces_ref):
    step = 16
    for h in range(0, DEVS, step):
        block = stage[h * 2 * HALF : (h + step) * 2 * HALF, :]
        pieces_ref[h : h + step] = block.reshape(step, 2 * HALF, LANES).astype(BF16)


def first_kernel(rows_ref, cols_ref, pair_ref, w_in_ref, w_gate_ref, pieces_ref, res_ref, gate_ref, stage):
    w = jnp.concatenate([w_in_ref[...].T, w_gate_ref[...].T], axis=0)
    mask_at = tile_mask(rows_ref, cols_ref)
    for s in range(0, HALF, 2):
        x = jnp.concatenate(
            [pair_ref[s], pair_ref[HALF + s], pair_ref[s + 1], pair_ref[HALF + s + 1]], axis=0
        )
        x = x.astype(F32).T
        lanes = slice(s * LANES, (s + 2) * LANES)
        gate_ref[:, lanes] = project(x, w, mask_at, s, 2, stage)
        res_ref[:, lanes] = x
    put_pieces(stage, pieces_ref)


def product_kernel(incoming, x_ref, out_ref, left, right):
    for at, whole in ((0, left), (HALF, right)):
        for pair in range(4):
            a = x_ref[:, 2 * pair, at : at + HALF, :].reshape(16 * HALF, LANES)
            b = x_ref[:, 2 * pair + 1, at : at + HALF, :].reshape(16 * HALF, LANES)
            top = jnp.concatenate([a[:, :COLS], b[:, :COLS]], axis=1)
            bottom = jnp.concatenate([a[:, COLS:], b[:, COLS:]], axis=1)
            lanes = slice(pair * LANES, (pair + 1) * LANES)
            whole[:, 0, :, lanes] = top.reshape(16, HALF, LANES)
            whole[:, 1, :, lanes] = bottom.reshape(16, HALF, LANES)
    lhs = left[...].reshape(512, 512)
    rhs = right[...].reshape(512, 512)
    dims = (((0,), (0,)), ((), ())) if incoming else (((1,), (1,)), ((), ()))
    mixed = lax.dot_general(lhs, rhs, dims, preferred_element_type=F32).astype(BF16)
    mixed = mixed.reshape(16, 2, HALF, 512)
    for pair in range(4):
        lanes = slice(pair * LANES, (pair + 1) * LANES)
        top = mixed[:, 0, :, lanes].reshape(16 * HALF, LANES)
        bottom = mixed[:, 1, :, lanes].reshape(16 * HALF, LANES)
        a = jnp.concatenate([top[:, :COLS], bottom[:, :COLS]], axis=1)
        b = jnp.concatenate([top[:, COLS:], bottom[:, COLS:]], axis=1)
        out_ref[:, 2 * pair] = a.reshape(16, HALF, LANES)
        out_ref[:, 2 * pair + 1] = b.reshape(16, HALF, LANES)


def scale_mixed(mixed_ref, scaled):
    total = jnp.zeros((HALF, LANES), F32)
    for h in range(128):
        total += mixed_ref[h].astype(F32)
    mean = total * (1.0 / 128)
    square = jnp.zeros((HALF, LANES), F32)
    for h in range(128):
        center = mixed_ref[h].astype(F32) - mean
        square += center * center
    factor = lax.rsqrt(jnp.maximum(square * (1.0 / 128), 1.0))
    for h in range(128):
        scaled[h * HALF : (h + 1) * HALF, :] = (mixed_ref[h].astype(F32) - mean) * factor


def finish(scaled, s, w_out, res_ref, gate_ref):
    lanes = slice(s * LANES, (s + 2) * LANES)
    both = jnp.concatenate(
        [scaled[pl.ds(s + n, 128, stride=HALF), :].astype(BF16) for n in range(2)], axis=1
    )
    update = jnp.dot(w_out, both, preferred_element_type=F32)
    return (res_ref[:, lanes] + gate_ref[:, lanes] * update).astype(BF16)


def middle_kernel(
    rows_ref, cols_ref, mixed_ref, res_ref, gate_ref, w_out_ref, w_in_ref, w_gate_ref,
    pieces_ref, next_res_ref, next_gate_ref, scaled, stage,
):
    w_out = w_out_ref[...].T
    w = jnp.concatenate([w_in_ref[...].T, w_gate_ref[...].T], axis=0)
    mask_at = tile_mask(rows_ref, cols_ref)
    scale_mixed(mixed_ref, scaled)
    for s in range(0, HALF, 2):
        x = finish(scaled, s, w_out, res_ref, gate_ref).astype(F32)
        lanes = slice(s * LANES, (s + 2) * LANES)
        next_gate_ref[:, lanes] = project(x, w, mask_at, s, 2, stage)
        next_res_ref[:, lanes] = x
    put_pieces(stage, pieces_ref)


def last_kernel(mixed_ref, res_ref, gate_ref, w_out_ref, up_ref, down_ref, out_ref, scaled):
    w_out = w_out_ref[...].T
    up = up_ref[...].T
    down = down_ref[...].T
    scale_mixed(mixed_ref, scaled)
    for s in range(0, HALF, 2):
        x = finish(scaled, s, w_out, res_ref, gate_ref).astype(F32)
        p = jnp.dot(up, normalize(x), preferred_element_type=F32)
        hidden = (p[:512] * sigmoid(p[:512]) * p[512:]).astype(BF16)
        y = x + jnp.dot(down, hidden, preferred_element_type=F32)
        y = y.T.astype(BF16)
        for n, at in enumerate((s, HALF + s, s + 1, HALF + s + 1)):
            out_ref[at] = y[n * COLS : (n + 1) * COLS]


SMEM = pl.BlockSpec(memory_space=pltpu.SMEM)
VMEM = pl.BlockSpec(memory_space=pltpu.VMEM)
PARAMS = pltpu.CompilerParams(vmem_limit_bytes=32 << 20)


def exchange(x):
    return lax.all_to_all(x, ("row", "col"), 0, 0, tiled=True)


def on_device(
    pair, residue_mask, out_in_w, out_gate_w, out_out_w, inc_in_w, inc_gate_w, inc_out_w,
    trans_up, trans_down,
):
    mask_cols = residue_mask.reshape(4, 128)
    pieces_t = jax.ShapeDtypeStruct((DEVS, 2 * HALF, LANES), BF16)
    mixed_t = jax.ShapeDtypeStruct((16, 8, HALF, LANES), BF16)
    wide_t = jax.ShapeDtypeStruct((CHANS, ROWS * COLS), F32)
    stage_t = pltpu.VMEM((DEVS * 2 * HALF, LANES), F32)
    scaled_t = pltpu.VMEM((DEVS * HALF, LANES), F32)
    whole_t = pltpu.VMEM((16, 2, HALF, 512), BF16)

    def product(incoming, pieces):
        mixed = pl.pallas_call(
            functools.partial(product_kernel, incoming),
            out_shape=mixed_t,
            in_specs=[VMEM],
            out_specs=VMEM,
            scratch_shapes=[whole_t, whole_t],
            compiler_params=PARAMS,
        )(pieces.reshape(16, 8, 2 * HALF, LANES))
        return mixed.reshape(DEVS, HALF, LANES)

    pieces, res, gate = pl.pallas_call(
        first_kernel,
        out_shape=(pieces_t, wide_t, wide_t),
        in_specs=[SMEM] + [VMEM] * 4,
        out_specs=(VMEM,) * 3,
        scratch_shapes=[stage_t],
        compiler_params=PARAMS,
    )(residue_mask, mask_cols, pair, out_in_w, out_gate_w)
    mixed = exchange(product(False, exchange(pieces)))
    pieces, res, gate = pl.pallas_call(
        middle_kernel,
        out_shape=(pieces_t, wide_t, wide_t),
        in_specs=[SMEM] + [VMEM] * 7,
        out_specs=(VMEM,) * 3,
        scratch_shapes=[scaled_t, stage_t],
        compiler_params=PARAMS,
    )(residue_mask, mask_cols, mixed, res, gate, out_out_w, inc_in_w, inc_gate_w)
    mixed = exchange(product(True, exchange(pieces)))
    return pl.pallas_call(
        last_kernel,
        out_shape=jax.ShapeDtypeStruct((ROWS, COLS, CHANS), BF16),
        in_specs=[VMEM] * 6,
        out_specs=VMEM,
        scratch_shapes=[scaled_t],
        compiler_params=PARAMS,
    )(mixed, res, gate, inc_out_w, trans_up, trans_down)


def solution(mesh):
    in_specs = (P("row", "col", None), P(), P(), P(), P(), P(), P(), P(), P(), P())
    out_specs = P("row", "col", None)
    return jax.shard_map(
        on_device, mesh=mesh, in_specs=in_specs, out_specs=out_specs, check_vma=False
    )
```

```python
import functools

import jax
import jax.numpy as jnp
from jax import lax
from jax.experimental import pallas as pl
from jax.experimental.pallas import tpu as pltpu
from jax.sharding import PartitionSpec as P

F32 = jnp.float32
BF16 = jnp.bfloat16
ROWS, COLS, CHANS = 32, 64, 128
HALF = ROWS // 2
LANES = 2 * COLS
SPOTS = ROWS * COLS
DEVS = 128
STAGE = 40
SCALED = 24


def tree(parts):
    while len(parts) > 1:
        parts = [a + b for a, b in zip(parts[::2], parts[1::2])]
    return parts[0]


def normalize(x):
    center = x - jnp.mean(x, axis=0, keepdims=True)
    spread = jnp.mean(center * center, axis=0, keepdims=True)
    return (center * lax.rsqrt(spread + 1e-05)).astype(BF16)


def put_mask(rows_ref, cols_ref, mask_ref):
    row0 = lax.axis_index("row") * ROWS
    col = lax.axis_index("col")
    line = cols_ref[pl.ds(col // 2, 1), :].astype(F32)
    swapped = pltpu.roll(line, COLS, 1)
    low = lax.broadcasted_iota(jnp.int32, (1, LANES), 1) < COLS
    cols = jnp.where(low == ((col % 2) == 0), line, swapped)
    for s in range(HALF):
        top = rows_ref[row0 + s].astype(F32)
        bottom = rows_ref[row0 + HALF + s].astype(F32)
        mask_ref[s : s + 1, :] = cols * jnp.where(low, top, bottom)


def project(x, w):
    return jnp.dot(w, normalize(x), preferred_element_type=F32)


def stage_operands(p, mask_ref, s0, count, stage):
    mask = jnp.concatenate([mask_ref[s0 + n : s0 + n + 1, :] for n in range(count)], axis=1)
    half_mask = 0.5 * mask
    for at, k in ((0, 0), (HALF, 256)):
        value = half_mask * p[k + 128 : k + 256]
        value = value * jnp.tanh(0.5 * p[k : k + 128]) + value
        for n in range(count):
            stage[pl.ds(at + s0 + n, DEVS, stride=STAGE), :] = value[:, n * LANES : (n + 1) * LANES]


def put_pieces(stage, pieces_ref):
    for h in range(DEVS):
        pieces_ref[h] = stage[h * STAGE : h * STAGE + 2 * HALF, :].astype(BF16)


def load_steps(pair_ref, s0, count):
    blocks = []
    for s in range(s0, s0 + count):
        blocks += [pair_ref[s], pair_ref[HALF + s]]
    return jnp.concatenate(blocks, axis=0).T


def first_kernel(
    rows_hbm, cols_hbm, pair_hbm, w_in_hbm, pieces_ref, mask_ref,
    rows_ref, cols_ref, pair_ref, w_in_ref, stage, sems,
):
    moves = ((pair_hbm, pair_ref), (w_in_hbm, w_in_ref), (cols_hbm, cols_ref), (rows_hbm, rows_ref))
    copies = [pltpu.make_async_copy(a, b, sems.at[n]) for n, (a, b) in enumerate(moves)]
    for copy in copies:
        copy.start()
    for copy in copies:
        copy.wait()
    put_mask(rows_ref, cols_ref, mask_ref)
    w = w_in_ref[...].T
    for s in range(0, HALF, 8):
        p = project(load_steps(pair_ref, s, 8).astype(F32), w)
        stage_operands(p, mask_ref, s, 8, stage)
    put_pieces(stage, pieces_ref)


def gate_kernel(from_pair, x_ref, w_gate_ref, gate_ref, *res_ref):
    w = w_gate_ref[...].T
    for s in range(0, HALF, 8):
        lanes = slice(s * LANES, (s + 8) * LANES)
        if from_pair:
            x = load_steps(x_ref, s, 8)
            res_ref[0][:, lanes] = x
        else:
            x = x_ref[:, lanes]
        gate_ref[:, lanes] = 0.5 * jnp.tanh(0.5 * project(x.astype(F32), w)) + 0.5


def product_kernel(incoming, x_ref, out_ref, left, right):
    for at, whole in ((0, left), (HALF, right)):
        for pair in range(4):
            a = x_ref[:, 2 * pair, at : at + HALF, :].reshape(16 * HALF, LANES)
            b = x_ref[:, 2 * pair + 1, at : at + HALF, :].reshape(16 * HALF, LANES)
            top = jnp.concatenate([a[:, :COLS], b[:, :COLS]], axis=1)
            bottom = jnp.concatenate([a[:, COLS:], b[:, COLS:]], axis=1)
            lanes = slice(pair * LANES, (pair + 1) * LANES)
            whole[:, 0, :, lanes] = top.reshape(16, HALF, LANES)
            whole[:, 1, :, lanes] = bottom.reshape(16, HALF, LANES)
    lhs = left[...].reshape(512, 512)
    rhs = right[...].reshape(512, 512)
    dims = (((0,), (0,)), ((), ())) if incoming else (((1,), (1,)), ((), ()))
    mixed = lax.dot_general(lhs, rhs, dims, preferred_element_type=F32).astype(BF16)
    mixed = mixed.reshape(16, 2, HALF, 512)
    for pair in range(4):
        lanes = slice(pair * LANES, (pair + 1) * LANES)
        top = mixed[:, 0, :, lanes].reshape(16 * HALF, LANES)
        bottom = mixed[:, 1, :, lanes].reshape(16 * HALF, LANES)
        a = jnp.concatenate([top[:, :COLS], bottom[:, :COLS]], axis=1)
        b = jnp.concatenate([top[:, COLS:], bottom[:, COLS:]], axis=1)
        out_ref[:, 2 * pair] = a.reshape(16, HALF, LANES)
        out_ref[:, 2 * pair + 1] = b.reshape(16, HALF, LANES)


def scale_mixed(mixed_ref, scaled):
    sums = [None] * 8
    for h in range(DEVS):
        value = mixed_ref[h].astype(F32)
        sums[h % 8] = value if h < 8 else sums[h % 8] + value
    mean = tree(sums) * (1.0 / 128)
    for h in range(DEVS):
        center = mixed_ref[h].astype(F32) - mean
        sums[h % 8] = center * center if h < 8 else sums[h % 8] + center * center
    factor = lax.rsqrt(jnp.maximum(tree(sums) * (1.0 / 128), 1.0))
    for h in range(DEVS):
        scaled[h * SCALED : h * SCALED + HALF, :] = (mixed_ref[h].astype(F32) - mean) * factor


def finish(scaled, s0, count, w_out, res_ref, gate_ref):
    lanes = slice(s0 * LANES, (s0 + count) * LANES)
    rows = [
        scaled[pl.ds(s0 + n, DEVS, stride=SCALED), :].astype(BF16) for n in range(count)
    ]
    update = jnp.dot(w_out, jnp.concatenate(rows, axis=1), preferred_element_type=F32)
    return (res_ref[:, lanes].astype(F32) + gate_ref[:, lanes] * update).astype(BF16)


def middle_kernel(
    mixed_ref, mask_ref, res_ref, gate_ref, w_out_ref, w_in_ref, pieces_ref, first_ref, scaled, stage
):
    w_out = w_out_ref[...].T
    w = w_in_ref[...].T
    scale_mixed(mixed_ref, scaled)
    for s in range(0, HALF, 8):
        x = finish(scaled, s, 8, w_out, res_ref, gate_ref)
        first_ref[:, s * LANES : (s + 8) * LANES] = x
        stage_operands(project(x.astype(F32), w), mask_ref, s, 8, stage)
    put_pieces(stage, pieces_ref)


def last_kernel(mixed_ref, res_ref, gate_ref, w_out_ref, up_ref, down_ref, out_ref, scaled):
    w_out = w_out_ref[...].T
    up = up_ref[...].T
    down = down_ref[...].T
    scale_mixed(mixed_ref, scaled)
    for s in range(0, HALF, 8):
        x = finish(scaled, s, 8, w_out, res_ref, gate_ref).astype(F32)
        p = project(x, up)
        half = 0.5 * p[:512]
        hidden = ((half * jnp.tanh(half) + half) * p[512:]).astype(BF16)
        y = x + jnp.dot(down, hidden, preferred_element_type=F32)
        y = y.astype(BF16).T
        for n in range(8):
            out_ref[s + n] = y[2 * n * COLS : (2 * n + 1) * COLS]
            out_ref[HALF + s + n] = y[(2 * n + 1) * COLS : (2 * n + 2) * COLS]


VMEM = pl.BlockSpec(memory_space=pltpu.VMEM)
ANY = pl.BlockSpec(memory_space=pl.ANY)
PIECES = jax.ShapeDtypeStruct((DEVS, 2 * HALF, LANES), BF16)
MASK = jax.ShapeDtypeStruct((HALF, LANES), F32)
MIXED = jax.ShapeDtypeStruct((16, 8, HALF, LANES), BF16)
GATE = jax.ShapeDtypeStruct((CHANS, SPOTS), F32)
RES = jax.ShapeDtypeStruct((CHANS, SPOTS), BF16)
TILE = jax.ShapeDtypeStruct((ROWS, COLS, CHANS), BF16)
STAGE_T = pltpu.VMEM((DEVS * STAGE, LANES), F32)
SCALED_T = pltpu.VMEM((DEVS * SCALED, LANES), F32)


def local(kernel, out, scratch, args, limit=32, flops=0, moved=0):
    return pl.pallas_call(
        kernel,
        out_shape=out,
        in_specs=[VMEM] * len(args),
        out_specs=jax.tree.map(lambda _: VMEM, out),
        scratch_shapes=scratch,
        compiler_params=pltpu.CompilerParams(vmem_limit_bytes=limit << 20),
        cost_estimate=pl.CostEstimate(flops=flops, bytes_accessed=moved, transcendentals=0),
    )(*args)


def first(residue_mask, pair, w_in):
    return pl.pallas_call(
        first_kernel,
        out_shape=(PIECES, MASK),
        in_specs=[ANY] * 4,
        out_specs=(VMEM, VMEM),
        scratch_shapes=[
            pltpu.SMEM((512,), jnp.int32),
            pltpu.VMEM((4, LANES), jnp.int32),
            pltpu.VMEM((ROWS, COLS, CHANS), BF16),
            pltpu.VMEM((CHANS, 512), BF16),
            STAGE_T,
            pltpu.SemaphoreType.DMA((4,)),
        ],
        compiler_params=pltpu.CompilerParams(vmem_limit_bytes=60 << 20),
    )(residue_mask, residue_mask.reshape(4, LANES), pair, w_in)


def gate_pair(pair, w_gate):
    kernel = functools.partial(gate_kernel, True)
    return local(kernel, (GATE, RES), [], (pair, w_gate), flops=1 << 28, moved=4 << 20)


def gate_first(x, w_gate):
    kernel = functools.partial(gate_kernel, False)
    return local(kernel, GATE, [], (x, w_gate), flops=1 << 28, moved=4 << 20)


def product(incoming, pieces):
    whole = pltpu.VMEM((16, 2, HALF, 512), BF16)
    kernel = functools.partial(product_kernel, incoming)
    mixed = local(kernel, MIXED, [whole, whole], (pieces.reshape(16, 8, 2 * HALF, LANES),))
    return mixed.reshape(DEVS, HALF, LANES)


def middle(*args):
    return local(middle_kernel, (PIECES, RES), [SCALED_T, STAGE_T], args)


def last(*args):
    return local(last_kernel, TILE, [SCALED_T], args)


def exchange(x):
    return lax.all_to_all(x, ("row", "col"), 0, 0, tiled=True)


def on_device(
    pair, residue_mask, out_in_w, out_gate_w, out_out_w, inc_in_w, inc_gate_w, inc_out_w,
    trans_up, trans_down,
):
    pieces, mask = first(residue_mask, pair, out_in_w)
    pair, pieces = lax.optimization_barrier((pair, pieces))
    gate, res = gate_pair(pair, out_gate_w)
    mixed = exchange(product(False, exchange(pieces)))
    pieces, res = middle(mixed, mask, res, gate, out_out_w, inc_in_w)
    gate = gate_first(res, inc_gate_w)
    mixed = exchange(product(True, exchange(pieces)))
    return last(mixed, res, gate, inc_out_w, trans_up, trans_down)


def solution(mesh):
    in_specs = (P("row", "col", None), P(), P(), P(), P(), P(), P(), P(), P(), P())
    out_specs = P("row", "col", None)
    return jax.shard_map(
        on_device, mesh=mesh, in_specs=in_specs, out_specs=out_specs, check_vma=False
    )
```

```python
import functools

import jax
import jax.numpy as jnp
from jax import lax
from jax.experimental import pallas as pl
from jax.experimental.pallas import tpu as pltpu
from jax.sharding import PartitionSpec as P

F32 = jnp.float32
BF16 = jnp.bfloat16
ROWS, COLS, CHANS = 32, 64, 128
HALF = ROWS // 2
LANES = 2 * COLS
SPOTS = ROWS * COLS
DEVS = 128
STAGE = 40
SCALED = 24


def tree(parts):
    while len(parts) > 1:
        parts = [a + b for a, b in zip(parts[::2], parts[1::2])]
    return parts[0]


def normalize(x):
    center = x - jnp.mean(x, axis=0, keepdims=True)
    spread = jnp.mean(center * center, axis=0, keepdims=True)
    return (center * lax.rsqrt(spread + 1e-05)).astype(BF16)


def sigmoid(x):
    return 0.5 * jnp.tanh(0.5 * x) + 0.5


def put_mask(present_ref, mask_ref):
    row0 = lax.axis_index("row") * ROWS
    col = lax.axis_index("col")
    lane = lax.broadcasted_iota(jnp.int32, (HALF, LANES), 1)
    step = lax.broadcasted_iota(jnp.int32, (HALF, LANES), 0)
    low = lane < COLS
    line = present_ref[pl.ds(col // 2, 1), :].astype(F32)
    cols = jnp.where(low == ((col % 2) == 0), line, pltpu.roll(line, COLS, 1))
    line = present_ref[pl.ds(row0 // LANES, 1), :].astype(F32)
    spot = lane - row0 % LANES
    top = jnp.sum(jnp.where(spot == step, line, 0.0), axis=1, keepdims=True)
    bottom = jnp.sum(jnp.where(spot == step + HALF, line, 0.0), axis=1, keepdims=True)
    mask_ref[...] = cols * jnp.where(low, top, bottom)


def project(x, w):
    return jnp.dot(w, normalize(x), preferred_element_type=F32)


def stage_operands(p, mask_ref, s0, count, stage):
    mask = jnp.concatenate([mask_ref[s0 + n : s0 + n + 1, :] for n in range(count)], axis=1)
    half_mask = 0.5 * mask
    for at, k in ((0, 0), (HALF, 256)):
        value = half_mask * p[k + 128 : k + 256]
        value = value * jnp.tanh(0.5 * p[k : k + 128]) + value
        for n in range(count):
            stage[pl.ds(at + s0 + n, DEVS, stride=STAGE), :] = value[:, n * LANES : (n + 1) * LANES]


def put_pieces(stage, pieces_ref):
    for h in range(DEVS):
        pieces_ref[h] = stage[h * STAGE : h * STAGE + 2 * HALF, :].astype(BF16)


def load_steps(pair_ref, s0, count):
    blocks = []
    for s in range(s0, s0 + count):
        blocks += [pair_ref[s], pair_ref[HALF + s]]
    return jnp.concatenate(blocks, axis=0).T


def first_kernel(
    pair_hbm, w_in_hbm, present_hbm, pieces_ref, mask_ref, pair_ref, w_in_ref, present_ref, stage, sems
):
    moves = ((pair_hbm, pair_ref), (w_in_hbm, w_in_ref), (present_hbm, present_ref))
    copies = [pltpu.make_async_copy(a, b, sems.at[n]) for n, (a, b) in enumerate(moves)]
    for copy in copies:
        copy.start()
    for copy in copies:
        copy.wait()
    put_mask(present_ref, mask_ref)
    w = w_in_ref[...].T
    for s in range(0, HALF, 8):
        p = project(load_steps(pair_ref, s, 8).astype(F32), w)
        stage_operands(p, mask_ref, s, 8, stage)
    put_pieces(stage, pieces_ref)


def side_kernel(
    pair_ref, gate_w_ref, out_w_ref, in_w_ref, next_gate_w_ref, next_out_w_ref, up_ref, down_ref,
    gate_ref, res_ref, out_t_ref, in_t_ref, next_out_t_ref, up_t_ref, down_t_ref,
):
    w = gate_w_ref[...].T
    for s in range(0, HALF, 8):
        lanes = slice(s * LANES, (s + 8) * LANES)
        x = load_steps(pair_ref, s, 8)
        res_ref[:, lanes] = x
        gate_ref[:, lanes] = sigmoid(project(x.astype(F32), w))
    out_t_ref[...] = out_w_ref[...].T
    in_t_ref[:512] = in_w_ref[...].T
    in_t_ref[512:] = next_gate_w_ref[...].T
    next_out_t_ref[...] = next_out_w_ref[...].T
    up_t_ref[...] = up_ref[...].T
    down_t_ref[...] = down_ref[...].T


def product_kernel(incoming, x_ref, out_ref, left, right):
    for at, whole in ((0, left), (HALF, right)):
        for pair in range(4):
            a = x_ref[:, 2 * pair, at : at + HALF, :].reshape(16 * HALF, LANES)
            b = x_ref[:, 2 * pair + 1, at : at + HALF, :].reshape(16 * HALF, LANES)
            top = jnp.concatenate([a[:, :COLS], b[:, :COLS]], axis=1)
            bottom = jnp.concatenate([a[:, COLS:], b[:, COLS:]], axis=1)
            lanes = slice(pair * LANES, (pair + 1) * LANES)
            whole[:, 0, :, lanes] = top.reshape(16, HALF, LANES)
            whole[:, 1, :, lanes] = bottom.reshape(16, HALF, LANES)
    lhs = left[...].reshape(512, 512)
    rhs = right[...].reshape(512, 512)
    dims = (((0,), (0,)), ((), ())) if incoming else (((1,), (1,)), ((), ()))
    mixed = lax.dot_general(lhs, rhs, dims, preferred_element_type=F32).astype(BF16)
    mixed = mixed.reshape(16, 2, HALF, 512)
    for pair in range(4):
        lanes = slice(pair * LANES, (pair + 1) * LANES)
        top = mixed[:, 0, :, lanes].reshape(16 * HALF, LANES)
        bottom = mixed[:, 1, :, lanes].reshape(16 * HALF, LANES)
        a = jnp.concatenate([top[:, :COLS], bottom[:, :COLS]], axis=1)
        b = jnp.concatenate([top[:, COLS:], bottom[:, COLS:]], axis=1)
        out_ref[:, 2 * pair] = a.reshape(16, HALF, LANES)
        out_ref[:, 2 * pair + 1] = b.reshape(16, HALF, LANES)


def scale_mixed(mixed_ref, scaled):
    sums = [None] * 8
    for h in range(DEVS):
        value = mixed_ref[h].astype(F32)
        sums[h % 8] = value if h < 8 else sums[h % 8] + value
    mean = tree(sums) * (1.0 / 128)
    for h in range(DEVS):
        center = mixed_ref[h].astype(F32) - mean
        sums[h % 8] = center * center if h < 8 else sums[h % 8] + center * center
    factor = lax.rsqrt(jnp.maximum(tree(sums) * (1.0 / 128), 1.0))
    for h in range(DEVS):
        scaled[h * SCALED : h * SCALED + HALF, :] = (mixed_ref[h].astype(F32) - mean) * factor


def finish(scaled, s0, count, w_out, res_ref, gate_ref):
    lanes = slice(s0 * LANES, (s0 + count) * LANES)
    rows = [
        scaled[pl.ds(s0 + n, DEVS, stride=SCALED), :].astype(BF16) for n in range(count)
    ]
    update = jnp.dot(w_out, jnp.concatenate(rows, axis=1), preferred_element_type=F32)
    return (res_ref[:, lanes].astype(F32) + gate_ref[:, lanes] * update).astype(BF16)


def middle_kernel(
    mixed_ref, mask_ref, res_ref, gate_ref, w_out_ref, w_in_ref,
    pieces_ref, first_ref, next_gate_ref, scaled, stage,
):
    scale_mixed(mixed_ref, scaled)
    for s in range(0, HALF, 8):
        lanes = slice(s * LANES, (s + 8) * LANES)
        x = finish(scaled, s, 8, w_out_ref[...], res_ref, gate_ref)
        first_ref[:, lanes] = x
        p = project(x.astype(F32), w_in_ref[...])
        stage_operands(p, mask_ref, s, 8, stage)
        next_gate_ref[:, lanes] = sigmoid(p[512:])
    put_pieces(stage, pieces_ref)


def last_kernel(mixed_ref, res_ref, gate_ref, w_out_ref, up_ref, down_ref, out_ref, scaled):
    scale_mixed(mixed_ref, scaled)
    x = finish(scaled, 0, HALF, w_out_ref[...], res_ref, gate_ref).astype(F32)
    p = project(x, up_ref[...])
    half = (0.5 * p[:512]).astype(BF16)
    hidden = (half * jnp.tanh(half) + half) * p[512:].astype(BF16)
    y = x + jnp.dot(down_ref[...], hidden, preferred_element_type=F32)
    y = y.astype(BF16).T
    for s in range(HALF):
        out_ref[s] = y[2 * s * COLS : (2 * s + 1) * COLS]
        out_ref[HALF + s] = y[(2 * s + 1) * COLS : (2 * s + 2) * COLS]


VMEM = pl.BlockSpec(memory_space=pltpu.VMEM)
ANY = pl.BlockSpec(memory_space=pl.ANY)
PIECES = jax.ShapeDtypeStruct((DEVS, 2 * HALF, LANES), BF16)
MASK = jax.ShapeDtypeStruct((HALF, LANES), F32)
MIXED = jax.ShapeDtypeStruct((16, 8, HALF, LANES), BF16)
GATE = jax.ShapeDtypeStruct((CHANS, SPOTS), F32)
RES = jax.ShapeDtypeStruct((CHANS, SPOTS), BF16)
TILE = jax.ShapeDtypeStruct((ROWS, COLS, CHANS), BF16)
STAGE_T = pltpu.VMEM((DEVS * STAGE, LANES), F32)
SCALED_T = pltpu.VMEM((DEVS * SCALED, LANES), F32)


def local(kernel, out, scratch, args, limit=32, flops=0, moved=0):
    return pl.pallas_call(
        kernel,
        out_shape=out,
        in_specs=[VMEM] * len(args),
        out_specs=jax.tree.map(lambda _: VMEM, out),
        scratch_shapes=scratch,
        compiler_params=pltpu.CompilerParams(vmem_limit_bytes=limit << 20),
        cost_estimate=pl.CostEstimate(flops=flops, bytes_accessed=moved, transcendentals=0),
    )(*args)


def first(residue_mask, pair, w_in):
    return pl.pallas_call(
        first_kernel,
        out_shape=(PIECES, MASK),
        in_specs=[ANY] * 3,
        out_specs=(VMEM, VMEM),
        scratch_shapes=[
            pltpu.VMEM((ROWS, COLS, CHANS), BF16),
            pltpu.VMEM((CHANS, 512), BF16),
            pltpu.VMEM((4, LANES), jnp.int32),
            STAGE_T,
            pltpu.SemaphoreType.DMA((3,)),
        ],
        compiler_params=pltpu.CompilerParams(vmem_limit_bytes=60 << 20),
    )(pair, w_in, residue_mask.reshape(4, LANES))


def weight(rows, cols=CHANS):
    return jax.ShapeDtypeStruct((rows, cols), BF16)


def side(*args):
    out = (GATE, RES, weight(128), weight(640), weight(128), weight(1024), weight(128, 512))
    return local(side_kernel, out, [], args, flops=1 << 28, moved=6 << 20)


def product(incoming, pieces):
    whole = pltpu.VMEM((16, 2, HALF, 512), BF16)
    kernel = functools.partial(product_kernel, incoming)
    mixed = local(kernel, MIXED, [whole, whole], (pieces.reshape(16, 8, 2 * HALF, LANES),))
    return mixed.reshape(DEVS, HALF, LANES)


def middle(*args):
    return local(middle_kernel, (PIECES, RES, GATE), [SCALED_T, STAGE_T], args)


def last(*args):
    return local(last_kernel, TILE, [SCALED_T], args)


def exchange(x):
    return lax.all_to_all(x, ("row", "col"), 0, 0, tiled=True)


def on_device(
    pair, residue_mask, out_in_w, out_gate_w, out_out_w, inc_in_w, inc_gate_w, inc_out_w,
    trans_up, trans_down,
):
    pieces, mask = first(residue_mask, pair, out_in_w)
    pair, pieces = lax.optimization_barrier((pair, pieces))
    beside = side(pair, out_gate_w, out_out_w, inc_in_w, inc_gate_w, inc_out_w, trans_up, trans_down)
    pieces, beside = lax.optimization_barrier((exchange(pieces), beside))
    gate, res, out_t, in_t, next_out_t, up_t, down_t = beside
    mixed = exchange(product(False, pieces))
    pieces, res, gate = middle(mixed, mask, res, gate, out_t, in_t)
    mixed = exchange(product(True, exchange(pieces)))
    return last(mixed, res, gate, next_out_t, up_t, down_t)


def solution(mesh):
    in_specs = (P("row", "col", None), P(), P(), P(), P(), P(), P(), P(), P(), P())
    out_specs = P("row", "col", None)
    return jax.shard_map(
        on_device, mesh=mesh, in_specs=in_specs, out_specs=out_specs, check_vma=False
    )
```

```python
import functools

import jax
import jax.numpy as jnp
from jax import lax
from jax.experimental import pallas as pl
from jax.experimental.pallas import tpu as pltpu
from jax.sharding import PartitionSpec as P

F32 = jnp.float32
BF16 = jnp.bfloat16
ROWS, COLS, CHANS = 32, 64, 128
HALF = ROWS // 2
LANES = 2 * COLS
SPOTS = ROWS * COLS
DEVS = 128
STAGE = 40
ROW_STEP = 24


def normalize(x):
    center = x - jnp.mean(x, axis=0, keepdims=True)
    spread = jnp.mean(center * center, axis=0, keepdims=True)
    return (center * lax.rsqrt(spread + 1e-05)).astype(BF16)


def sigmoid(x):
    return 0.5 * jnp.tanh(0.5 * x) + 0.5


def put_mask(present_ref, mask_ref):
    row0 = lax.axis_index("row") * ROWS
    col = lax.axis_index("col")
    lane = lax.broadcasted_iota(jnp.int32, (HALF, LANES), 1)
    step = lax.broadcasted_iota(jnp.int32, (HALF, LANES), 0)
    low = lane < COLS
    line = present_ref[pl.ds(col // 2, 1), :].astype(F32)
    cols = jnp.where(low == ((col % 2) == 0), line, pltpu.roll(line, COLS, 1))
    line = present_ref[pl.ds(row0 // LANES, 1), :].astype(F32)
    spot = lane - row0 % LANES
    top = jnp.sum(jnp.where(spot == step, line, 0.0), axis=1, keepdims=True)
    bottom = jnp.sum(jnp.where(spot == step + HALF, line, 0.0), axis=1, keepdims=True)
    mask_ref[...] = cols * jnp.where(low, top, bottom)


def project(x, w):
    return jnp.dot(w, normalize(x), preferred_element_type=F32)


def stage_operands(p, mask_ref, stage):
    half_mask = 0.5 * jnp.concatenate([mask_ref[s : s + 1, :] for s in range(HALF)], axis=1)
    for at, k in ((0, 0), (HALF, 256)):
        value = half_mask * p[k + 128 : k + 256]
        value = value * jnp.tanh(0.5 * p[k : k + 128]) + value
        for s in range(HALF):
            stage[pl.ds(at + s, DEVS, stride=STAGE), :] = value[:, s * LANES : (s + 1) * LANES]


def put_pieces(stage, pieces_ref):
    for h in range(DEVS):
        pieces_ref[h] = stage[h * STAGE : h * STAGE + 2 * HALF, :].astype(BF16)


def load_steps(pair_ref, s0, count):
    blocks = []
    for s in range(s0, s0 + count):
        blocks += [pair_ref[s], pair_ref[HALF + s]]
    return jnp.concatenate(blocks, axis=0).T


def first_kernel(
    pair_hbm, w_in_hbm, present_hbm, pieces_ref, mask_ref, pair_ref, w_in_ref, present_ref, stage, sems
):
    moves = ((pair_hbm, pair_ref), (w_in_hbm, w_in_ref), (present_hbm, present_ref))
    copies = [pltpu.make_async_copy(a, b, sems.at[n]) for n, (a, b) in enumerate(moves)]
    for copy in copies:
        copy.start()
    for copy in copies:
        copy.wait()
    put_mask(present_ref, mask_ref)
    w = w_in_ref[...].T
    p = project(load_steps(pair_ref, 0, HALF).astype(F32), w)
    stage_operands(p, mask_ref, stage)
    put_pieces(stage, pieces_ref)


def side_kernel(
    pair_ref, gate_w_ref, out_w_ref, in_w_ref, next_gate_w_ref, next_out_w_ref, up_ref, down_ref,
    gate_ref, res_ref, out_t_ref, in_t_ref, next_out_t_ref, up_t_ref, down_t_ref,
):
    w = gate_w_ref[...].T
    for s in range(0, HALF, 8):
        lanes = slice(s * LANES, (s + 8) * LANES)
        x = load_steps(pair_ref, s, 8)
        res_ref[:, lanes] = x
        gate_ref[:, lanes] = sigmoid(project(x.astype(F32), w))
    out_t_ref[...] = out_w_ref[...].T
    in_t_ref[:512] = in_w_ref[...].T
    in_t_ref[512:] = next_gate_w_ref[...].T
    next_out_t_ref[...] = next_out_w_ref[...].T
    up_t_ref[...] = up_ref[...].T
    down_t_ref[...] = down_ref[...].T


def product_kernel(incoming, x_ref, out_ref, left, right):
    for at, whole in ((0, left), (HALF, right)):
        for pair in range(4):
            a = x_ref[:, 2 * pair, at : at + HALF, :].reshape(16 * HALF, LANES)
            b = x_ref[:, 2 * pair + 1, at : at + HALF, :].reshape(16 * HALF, LANES)
            top = jnp.concatenate([a[:, :COLS], b[:, :COLS]], axis=1)
            bottom = jnp.concatenate([a[:, COLS:], b[:, COLS:]], axis=1)
            lanes = slice(pair * LANES, (pair + 1) * LANES)
            whole[:, 0, :, lanes] = top.reshape(16, HALF, LANES)
            whole[:, 1, :, lanes] = bottom.reshape(16, HALF, LANES)
    lhs = left[...].reshape(512, 512)
    rhs = right[...].reshape(512, 512)
    dims = (((0,), (0,)), ((), ())) if incoming else (((1,), (1,)), ((), ()))
    mixed = lax.dot_general(lhs, rhs, dims, preferred_element_type=F32).astype(BF16)
    mixed = mixed.reshape(16, 2, HALF, 512)
    for pair in range(4):
        lanes = slice(pair * LANES, (pair + 1) * LANES)
        top = mixed[:, 0, :, lanes].reshape(16 * HALF, LANES)
        bottom = mixed[:, 1, :, lanes].reshape(16 * HALF, LANES)
        a = jnp.concatenate([top[:, :COLS], bottom[:, :COLS]], axis=1)
        b = jnp.concatenate([top[:, COLS:], bottom[:, COLS:]], axis=1)
        out_ref[:, 2 * pair] = a.reshape(16, HALF, LANES)
        out_ref[:, 2 * pair + 1] = b.reshape(16, HALF, LANES)


def unpack(mixed_ref, rows):
    for h in range(DEVS):
        rows[h * ROW_STEP : h * ROW_STEP + HALF, :] = mixed_ref[h].astype(F32)


def scaled_step(rows, s):
    value = rows[pl.ds(s, DEVS, stride=ROW_STEP), :]
    center = value - jnp.mean(value, axis=0, keepdims=True)
    spread = jnp.mean(center * center, axis=0, keepdims=True)
    return (center * lax.rsqrt(jnp.maximum(spread, 1.0))).astype(BF16)


def finish(rows, s0, count, w_out, res_ref, gate_ref):
    lanes = slice(s0 * LANES, (s0 + count) * LANES)
    scaled = jnp.concatenate([scaled_step(rows, s0 + n) for n in range(count)], axis=1)
    update = jnp.dot(w_out, scaled, preferred_element_type=F32)
    return (res_ref[:, lanes].astype(F32) + gate_ref[:, lanes] * update).astype(BF16)


def middle_kernel(
    mixed_ref, mask_ref, res_ref, gate_ref, w_out_ref, w_in_ref,
    pieces_ref, first_ref, next_gate_ref, rows, stage,
):
    unpack(mixed_ref, rows)
    x = finish(rows, 0, HALF, w_out_ref[...], res_ref, gate_ref)
    first_ref[...] = x
    p = project(x.astype(F32), w_in_ref[...])
    stage_operands(p, mask_ref, stage)
    next_gate_ref[...] = sigmoid(p[512:])
    put_pieces(stage, pieces_ref)


def last_kernel(mixed_ref, res_ref, gate_ref, w_out_ref, up_ref, down_ref, out_ref, rows):
    unpack(mixed_ref, rows)
    starts = range(0, HALF, 8)
    tiles = [finish(rows, s, 8, w_out_ref[...], res_ref, gate_ref) for s in starts]
    for s, x in zip(starts, tiles):
        x = x.astype(F32)
        p = project(x, up_ref[...])
        half = (0.5 * p[:512]).astype(BF16)
        hidden = (half * jnp.tanh(half) + half) * p[512:].astype(BF16)
        y = x + jnp.dot(down_ref[...], hidden, preferred_element_type=F32)
        y = y.astype(BF16).T
        for n in range(8):
            out_ref[s + n] = y[2 * n * COLS : (2 * n + 1) * COLS]
            out_ref[HALF + s + n] = y[(2 * n + 1) * COLS : (2 * n + 2) * COLS]


VMEM = pl.BlockSpec(memory_space=pltpu.VMEM)
ANY = pl.BlockSpec(memory_space=pl.ANY)
PIECES = jax.ShapeDtypeStruct((DEVS, 2 * HALF, LANES), BF16)
MASK = jax.ShapeDtypeStruct((HALF, LANES), F32)
MIXED = jax.ShapeDtypeStruct((16, 8, HALF, LANES), BF16)
GATE = jax.ShapeDtypeStruct((CHANS, SPOTS), F32)
RES = jax.ShapeDtypeStruct((CHANS, SPOTS), BF16)
TILE = jax.ShapeDtypeStruct((ROWS, COLS, CHANS), BF16)
STAGE_T = pltpu.VMEM(((DEVS + 1) * STAGE, LANES), F32)
ROWS_T = pltpu.VMEM(((DEVS + 1) * ROW_STEP, LANES), F32)


def local(kernel, out, scratch, args, limit=32, flops=0, moved=0):
    return pl.pallas_call(
        kernel,
        out_shape=out,
        in_specs=[VMEM] * len(args),
        out_specs=jax.tree.map(lambda _: VMEM, out),
        scratch_shapes=scratch,
        compiler_params=pltpu.CompilerParams(vmem_limit_bytes=limit << 20),
        cost_estimate=pl.CostEstimate(flops=flops, bytes_accessed=moved, transcendentals=0),
    )(*args)


def first(residue_mask, pair, w_in):
    return pl.pallas_call(
        first_kernel,
        out_shape=(PIECES, MASK),
        in_specs=[ANY] * 3,
        out_specs=(VMEM, VMEM),
        scratch_shapes=[
            pltpu.VMEM((ROWS, COLS, CHANS), BF16),
            pltpu.VMEM((CHANS, 512), BF16),
            pltpu.VMEM((4, LANES), jnp.int32),
            STAGE_T,
            pltpu.SemaphoreType.DMA((3,)),
        ],
        compiler_params=pltpu.CompilerParams(vmem_limit_bytes=60 << 20),
    )(pair, w_in, residue_mask.reshape(4, LANES))


def weight(rows, cols=CHANS):
    return jax.ShapeDtypeStruct((rows, cols), BF16)


def side(*args):
    out = (GATE, RES, weight(128), weight(640), weight(128), weight(1024), weight(128, 512))
    return local(side_kernel, out, [], args, flops=1 << 28, moved=6 << 20)


def product(incoming, pieces):
    whole = pltpu.VMEM((16, 2, HALF, 512), BF16)
    kernel = functools.partial(product_kernel, incoming)
    mixed = local(kernel, MIXED, [whole, whole], (pieces.reshape(16, 8, 2 * HALF, LANES),))
    return mixed.reshape(DEVS, HALF, LANES)


def middle(*args):
    return local(middle_kernel, (PIECES, RES, GATE), [ROWS_T, STAGE_T], args)


def last(*args):
    return local(last_kernel, TILE, [ROWS_T], args)


def exchange(x):
    return lax.all_to_all(x, ("row", "col"), 0, 0, tiled=True)


def on_device(
    pair, residue_mask, out_in_w, out_gate_w, out_out_w, inc_in_w, inc_gate_w, inc_out_w,
    trans_up, trans_down,
):
    pieces, mask = first(residue_mask, pair, out_in_w)
    pair, pieces = lax.optimization_barrier((pair, pieces))
    beside = side(pair, out_gate_w, out_out_w, inc_in_w, inc_gate_w, inc_out_w, trans_up, trans_down)
    pieces, beside = lax.optimization_barrier((exchange(pieces), beside))
    gate, res, out_t, in_t, next_out_t, up_t, down_t = beside
    mixed = exchange(product(False, pieces))
    pieces, res, gate = middle(mixed, mask, res, gate, out_t, in_t)
    mixed = exchange(product(True, exchange(pieces)))
    return last(mixed, res, gate, next_out_t, up_t, down_t)


def solution(mesh):
    in_specs = (P("row", "col", None), P(), P(), P(), P(), P(), P(), P(), P(), P())
    out_specs = P("row", "col", None)
    return jax.shard_map(
        on_device, mesh=mesh, in_specs=in_specs, out_specs=out_specs, check_vma=False
    )
```

```python
import functools

import jax
import jax.numpy as jnp
from jax import lax
from jax.experimental import pallas as pl
from jax.experimental.pallas import tpu as pltpu
from jax.sharding import PartitionSpec as P

F32 = jnp.float32
BF16 = jnp.bfloat16
ROWS, COLS, CHANS = 32, 64, 128
HALF = ROWS // 2
LANES = 2 * COLS
SPOTS = ROWS * COLS
DEVS = 128
NATURAL = tuple(range(DEVS))


def far_first():
    def place(device):
        row, col = divmod(device, 8)
        at = (row // 4, col % 2 * 2 + row // 2 % 2, col // 2)
        return sum(min(k, 4 - k) for k in at), at, row % 2

    return tuple(sorted(range(DEVS), key=place, reverse=True))


FAR_FIRST = far_first()
STAGE = 40
ROW_STEP = 24


def normalize(x):
    center = x - jnp.mean(x, axis=0, keepdims=True)
    spread = jnp.mean(center * center, axis=0, keepdims=True)
    return (center * lax.rsqrt(spread + 1e-05)).astype(BF16)


def sigmoid(x):
    return 0.5 * jnp.tanh(0.5 * x) + 0.5


def put_mask(present_ref, mask_ref):
    row0 = lax.axis_index("row") * ROWS
    col = lax.axis_index("col")
    lane = lax.broadcasted_iota(jnp.int32, (HALF, LANES), 1)
    step = lax.broadcasted_iota(jnp.int32, (HALF, LANES), 0)
    low = lane < COLS
    line = present_ref[pl.ds(col // 2, 1), :].astype(F32)
    cols = jnp.where(low == ((col % 2) == 0), line, pltpu.roll(line, COLS, 1))
    line = present_ref[pl.ds(row0 // LANES, 1), :].astype(F32)
    spot = lane - row0 % LANES
    top = jnp.sum(jnp.where(spot == step, line, 0.0), axis=1, keepdims=True)
    bottom = jnp.sum(jnp.where(spot == step + HALF, line, 0.0), axis=1, keepdims=True)
    mask_ref[...] = cols * jnp.where(low, top, bottom)


def project(x, w):
    return jnp.dot(w, normalize(x), preferred_element_type=F32)


def stage_operands(p, mask_ref, stage):
    half_mask = 0.5 * jnp.concatenate([mask_ref[s : s + 1, :] for s in range(HALF)], axis=1)
    for at, k in ((0, 0), (HALF, 256)):
        value = half_mask * p[k + 128 : k + 256]
        value = value * jnp.tanh(0.5 * p[k : k + 128]) + value
        for s in range(HALF):
            stage[pl.ds(at + s, DEVS, stride=STAGE), :] = value[:, s * LANES : (s + 1) * LANES]


def put_pieces(stage, pieces_ref):
    for h in range(DEVS):
        pieces_ref[h] = stage[h * STAGE : h * STAGE + 2 * HALF, :].astype(BF16)


def load_steps(pair_ref, s0, count):
    blocks = []
    for s in range(s0, s0 + count):
        blocks += [pair_ref[s], pair_ref[HALF + s]]
    return jnp.concatenate(blocks, axis=0).T


def first_kernel(
    pair_hbm, w_in_hbm, present_hbm, pieces_ref, mask_ref, pair_ref, w_in_ref, present_ref, stage, sems
):
    moves = ((pair_hbm, pair_ref), (w_in_hbm, w_in_ref), (present_hbm, present_ref))
    copies = [pltpu.make_async_copy(a, b, sems.at[n]) for n, (a, b) in enumerate(moves)]
    for copy in copies:
        copy.start()
    for copy in copies:
        copy.wait()
    put_mask(present_ref, mask_ref)
    w = w_in_ref[...].T
    p = project(load_steps(pair_ref, 0, HALF).astype(F32), w)
    stage_operands(p, mask_ref, stage)
    put_pieces(stage, pieces_ref)


def side_kernel(
    pair_ref, gate_w_ref, out_w_ref, in_w_ref, next_gate_w_ref, next_out_w_ref, up_ref, down_ref,
    gate_ref, res_ref, out_t_ref, in_t_ref, next_out_t_ref, up_t_ref, down_t_ref, channels, ordered,
):
    w = gate_w_ref[...].T
    for s in range(0, HALF, 8):
        lanes = slice(s * LANES, (s + 8) * LANES)
        x = load_steps(pair_ref, s, 8)
        res_ref[:, lanes] = x
        gate_ref[:, lanes] = sigmoid(project(x.astype(F32), w))
    out_t_ref[...] = out_w_ref[...].T
    in_t_ref[:512] = in_w_ref[...].T
    in_t_ref[512:] = next_gate_w_ref[...].T
    channels[...] = next_out_w_ref[...].astype(F32)
    for n, channel in enumerate(FAR_FIRST):
        ordered[n : n + 1, :] = channels[channel : channel + 1, :]
    next_out_t_ref[...] = ordered[...].T.astype(BF16)
    up_t_ref[...] = up_ref[...].T
    down_t_ref[...] = down_ref[...].T


def product_kernel(incoming, order, x_ref, out_ref, left, right):
    for at, whole in ((0, left), (HALF, right)):
        for pair in range(4):
            a = x_ref[:, 2 * pair, at : at + HALF, :].reshape(16 * HALF, LANES)
            b = x_ref[:, 2 * pair + 1, at : at + HALF, :].reshape(16 * HALF, LANES)
            top = jnp.concatenate([a[:, :COLS], b[:, :COLS]], axis=1)
            bottom = jnp.concatenate([a[:, COLS:], b[:, COLS:]], axis=1)
            lanes = slice(pair * LANES, (pair + 1) * LANES)
            whole[:, 0, :, lanes] = top.reshape(16, HALF, LANES)
            whole[:, 1, :, lanes] = bottom.reshape(16, HALF, LANES)
    lhs = left[...].reshape(512, 512)
    rhs = right[...].reshape(512, 512)
    dims = (((0,), (0,)), ((), ())) if incoming else (((1,), (1,)), ((), ()))
    mixed = lax.dot_general(lhs, rhs, dims, preferred_element_type=F32).astype(BF16)
    mixed = mixed.reshape(16, 2, HALF, 512)
    for pair in range(4):
        lanes = slice(pair * LANES, (pair + 1) * LANES)
        top = mixed[:, 0, :, lanes].reshape(16 * HALF, LANES)
        bottom = mixed[:, 1, :, lanes].reshape(16 * HALF, LANES)
        a = jnp.concatenate([top[:, :COLS], bottom[:, :COLS]], axis=1)
        b = jnp.concatenate([top[:, COLS:], bottom[:, COLS:]], axis=1)
        for row in range(16):
            tile = slice(row * HALF, (row + 1) * HALF)
            out_ref[order.index(row * 8 + 2 * pair)] = a[tile]
            out_ref[order.index(row * 8 + 2 * pair + 1)] = b[tile]


def unpack(mixed_ref, rows):
    for h in range(DEVS):
        rows[h * ROW_STEP : h * ROW_STEP + HALF, :] = mixed_ref[h].astype(F32)


def scaled_step(rows, s):
    value = rows[pl.ds(s, DEVS, stride=ROW_STEP), :]
    center = value - jnp.mean(value, axis=0, keepdims=True)
    spread = jnp.mean(center * center, axis=0, keepdims=True)
    return (center * lax.rsqrt(jnp.maximum(spread, 1.0))).astype(BF16)


def finish(rows, s0, count, w_out, res_ref, gate_ref):
    lanes = slice(s0 * LANES, (s0 + count) * LANES)
    scaled = jnp.concatenate([scaled_step(rows, s0 + n) for n in range(count)], axis=1)
    update = jnp.dot(w_out, scaled, preferred_element_type=F32)
    return (res_ref[:, lanes].astype(F32) + gate_ref[:, lanes] * update).astype(BF16)


def middle_kernel(
    mixed_ref, mask_ref, res_ref, gate_ref, w_out_ref, w_in_ref,
    pieces_ref, first_ref, next_gate_ref, rows, stage,
):
    unpack(mixed_ref, rows)
    x = finish(rows, 0, HALF, w_out_ref[...], res_ref, gate_ref)
    first_ref[...] = x
    p = project(x.astype(F32), w_in_ref[...])
    stage_operands(p, mask_ref, stage)
    next_gate_ref[...] = sigmoid(p[512:])
    put_pieces(stage, pieces_ref)


def last_kernel(mixed_ref, res_ref, gate_ref, w_out_ref, up_ref, down_ref, out_ref, rows):
    unpack(mixed_ref, rows)
    starts = range(0, HALF, 8)
    tiles = [finish(rows, s, 8, w_out_ref[...], res_ref, gate_ref) for s in starts]
    for s, x in zip(starts, tiles):
        x = x.astype(F32)
        p = project(x, up_ref[...])
        half = (0.5 * p[:512]).astype(BF16)
        hidden = (half * jnp.tanh(half) + half) * p[512:].astype(BF16)
        y = x + jnp.dot(down_ref[...], hidden, preferred_element_type=F32)
        y = y.astype(BF16).T
        for n in range(8):
            out_ref[s + n] = y[2 * n * COLS : (2 * n + 1) * COLS]
            out_ref[HALF + s + n] = y[(2 * n + 1) * COLS : (2 * n + 2) * COLS]


VMEM = pl.BlockSpec(memory_space=pltpu.VMEM)
ANY = pl.BlockSpec(memory_space=pl.ANY)
PIECES = jax.ShapeDtypeStruct((DEVS, 2 * HALF, LANES), BF16)
MASK = jax.ShapeDtypeStruct((HALF, LANES), F32)
MIXED = jax.ShapeDtypeStruct((DEVS, HALF, LANES), BF16)
GATE = jax.ShapeDtypeStruct((CHANS, SPOTS), F32)
RES = jax.ShapeDtypeStruct((CHANS, SPOTS), BF16)
TILE = jax.ShapeDtypeStruct((ROWS, COLS, CHANS), BF16)
STAGE_T = pltpu.VMEM(((DEVS + 1) * STAGE, LANES), F32)
ROWS_T = pltpu.VMEM(((DEVS + 1) * ROW_STEP, LANES), F32)


def local(kernel, out, scratch, args, limit=32, flops=0, moved=0):
    return pl.pallas_call(
        kernel,
        out_shape=out,
        in_specs=[VMEM] * len(args),
        out_specs=jax.tree.map(lambda _: VMEM, out),
        scratch_shapes=scratch,
        compiler_params=pltpu.CompilerParams(vmem_limit_bytes=limit << 20),
        cost_estimate=pl.CostEstimate(flops=flops, bytes_accessed=moved, transcendentals=0),
    )(*args)


def first(residue_mask, pair, w_in):
    return pl.pallas_call(
        first_kernel,
        out_shape=(PIECES, MASK),
        in_specs=[ANY] * 3,
        out_specs=(VMEM, VMEM),
        scratch_shapes=[
            pltpu.VMEM((ROWS, COLS, CHANS), BF16),
            pltpu.VMEM((CHANS, 512), BF16),
            pltpu.VMEM((4, LANES), jnp.int32),
            STAGE_T,
            pltpu.SemaphoreType.DMA((3,)),
        ],
        compiler_params=pltpu.CompilerParams(vmem_limit_bytes=60 << 20),
    )(pair, w_in, residue_mask.reshape(4, LANES))


def weight(rows, cols=CHANS):
    return jax.ShapeDtypeStruct((rows, cols), BF16)


def side(*args):
    out = (GATE, RES, weight(128), weight(640), weight(128), weight(1024), weight(128, 512))
    channels = pltpu.VMEM((DEVS, CHANS), F32)
    return local(side_kernel, out, [channels, channels], args, flops=1 << 28, moved=6 << 20)


def product(incoming, order, pieces):
    whole = pltpu.VMEM((16, 2, HALF, 512), BF16)
    kernel = functools.partial(product_kernel, incoming, order)
    return local(kernel, MIXED, [whole, whole], (pieces.reshape(16, 8, 2 * HALF, LANES),))


def middle(*args):
    return local(middle_kernel, (PIECES, RES, GATE), [ROWS_T, STAGE_T], args)


def last(*args):
    return local(last_kernel, TILE, [ROWS_T], args)


def exchange(x, order=NATURAL):
    groups = None if order == NATURAL else [list(order)]
    return lax.all_to_all(x, ("row", "col"), 0, 0, axis_index_groups=groups, tiled=True)


def on_device(
    pair, residue_mask, out_in_w, out_gate_w, out_out_w, inc_in_w, inc_gate_w, inc_out_w,
    trans_up, trans_down,
):
    pieces, mask = first(residue_mask, pair, out_in_w)
    pair, pieces = lax.optimization_barrier((pair, pieces))
    beside = side(pair, out_gate_w, out_out_w, inc_in_w, inc_gate_w, inc_out_w, trans_up, trans_down)
    pieces, beside = lax.optimization_barrier((exchange(pieces), beside))
    gate, res, out_t, in_t, next_out_t, up_t, down_t = beside
    mixed = exchange(product(False, NATURAL, pieces))
    pieces, res, gate = middle(mixed, mask, res, gate, out_t, in_t)
    mixed = exchange(product(True, FAR_FIRST, exchange(pieces)), FAR_FIRST)
    return last(mixed, res, gate, next_out_t, up_t, down_t)


def solution(mesh):
    in_specs = (P("row", "col", None), P(), P(), P(), P(), P(), P(), P(), P(), P())
    out_specs = P("row", "col", None)
    return jax.shard_map(
        on_device, mesh=mesh, in_specs=in_specs, out_specs=out_specs, check_vma=False
    )
```

```python
import functools

import jax
import jax.numpy as jnp
from jax import lax
from jax.experimental import pallas as pl
from jax.experimental.pallas import tpu as pltpu
from jax.sharding import PartitionSpec as P

F32 = jnp.float32
BF16 = jnp.bfloat16
ROWS, COLS, CHANS = 32, 64, 128
HALF = ROWS // 2
LANES = 2 * COLS
SPOTS = ROWS * COLS
DEVS = 128
NATURAL = tuple(range(DEVS))


def far_first():
    def place(device):
        row, col = divmod(device, 8)
        at = (row // 4, col % 2 * 2 + row // 2 % 2, col // 2)
        return sum(min(k, 4 - k) for k in at), at, row % 2

    return tuple(sorted(range(DEVS), key=place, reverse=True))


FAR_FIRST = far_first()
STAGE = 40
ROW_STEP = 24


def normalize(x):
    center = x - jnp.mean(x, axis=0, keepdims=True)
    spread = jnp.mean(center * center, axis=0, keepdims=True)
    return (center * lax.rsqrt(spread + 1e-05)).astype(BF16)


def sigmoid(x):
    return 0.5 * jnp.tanh(0.5 * x) + 0.5


def put_mask(present_ref, mask_ref):
    row0 = lax.axis_index("row") * ROWS
    col = lax.axis_index("col")
    lane = lax.broadcasted_iota(jnp.int32, (HALF, LANES), 1)
    step = lax.broadcasted_iota(jnp.int32, (HALF, LANES), 0)
    low = lane < COLS
    line = present_ref[pl.ds(col // 2, 1), :].astype(F32)
    cols = jnp.where(low == ((col % 2) == 0), line, pltpu.roll(line, COLS, 1))
    line = present_ref[pl.ds(row0 // LANES, 1), :].astype(F32)
    spot = lane - row0 % LANES
    top = jnp.sum(jnp.where(spot == step, line, 0.0), axis=1, keepdims=True)
    bottom = jnp.sum(jnp.where(spot == step + HALF, line, 0.0), axis=1, keepdims=True)
    mask_ref[...] = cols * jnp.where(low, top, bottom)


def project(x, w):
    return jnp.dot(w, normalize(x), preferred_element_type=F32)


def stage_operands(p, mask_ref, stage, s0=0):
    steps = range(s0, s0 + p.shape[1] // LANES)
    half_mask = 0.5 * jnp.concatenate([mask_ref[s : s + 1, :] for s in steps], axis=1)
    for at, k in ((0, 0), (HALF, 256)):
        value = half_mask * p[k + 128 : k + 256]
        value = value * jnp.tanh(0.5 * p[k : k + 128]) + value
        for n, s in enumerate(steps):
            stage[pl.ds(at + s, DEVS, stride=STAGE), :] = value[:, n * LANES : (n + 1) * LANES]


def put_pieces(stage, pieces_ref):
    for h in range(DEVS):
        pieces_ref[h] = stage[h * STAGE : h * STAGE + 2 * HALF, :].astype(BF16)


def load_steps(pair_ref, s0, count):
    blocks = []
    for s in range(s0, s0 + count):
        blocks += [pair_ref[s], pair_ref[HALF + s]]
    return jnp.concatenate(blocks, axis=0).T


def first_kernel(
    pair_hbm, w_in_hbm, present_hbm, pieces_ref, mask_ref, pair_ref, w_in_ref, present_ref, stage, sems
):
    moves = ((pair_hbm, pair_ref), (w_in_hbm, w_in_ref), (present_hbm, present_ref))
    copies = [pltpu.make_async_copy(a, b, sems.at[n]) for n, (a, b) in enumerate(moves)]
    for copy in copies:
        copy.start()
    for copy in copies:
        copy.wait()
    put_mask(present_ref, mask_ref)
    w = w_in_ref[...].T
    p = project(load_steps(pair_ref, 0, HALF).astype(F32), w)
    stage_operands(p, mask_ref, stage)
    put_pieces(stage, pieces_ref)


def side_kernel(
    pair_ref, gate_w_ref, out_w_ref, in_w_ref, next_gate_w_ref, next_out_w_ref, up_ref, down_ref,
    gate_ref, res_ref, out_t_ref, in_t_ref, next_out_t_ref, up_t_ref, down_t_ref, channels, ordered,
):
    w = gate_w_ref[...].T
    for s in range(0, HALF, 8):
        lanes = slice(s * LANES, (s + 8) * LANES)
        x = load_steps(pair_ref, s, 8)
        res_ref[:, lanes] = x
        gate_ref[:, lanes] = sigmoid(project(x.astype(F32), w))
    out_t_ref[...] = out_w_ref[...].T
    in_t_ref[:512] = in_w_ref[...].T
    in_t_ref[512:] = next_gate_w_ref[...].T
    channels[...] = next_out_w_ref[...].astype(F32)
    for n, channel in enumerate(FAR_FIRST):
        ordered[n : n + 1, :] = channels[channel : channel + 1, :]
    next_out_t_ref[...] = ordered[...].T.astype(BF16)
    up_t_ref[...] = up_ref[...].T
    down_t_ref[...] = down_ref[...].T


def product_kernel(incoming, order, x_ref, out_ref, left, right):
    for at, whole in ((0, left), (HALF, right)):
        for pair in range(4):
            a = x_ref[:, 2 * pair, at : at + HALF, :].reshape(16 * HALF, LANES)
            b = x_ref[:, 2 * pair + 1, at : at + HALF, :].reshape(16 * HALF, LANES)
            top = jnp.concatenate([a[:, :COLS], b[:, :COLS]], axis=1)
            bottom = jnp.concatenate([a[:, COLS:], b[:, COLS:]], axis=1)
            lanes = slice(pair * LANES, (pair + 1) * LANES)
            whole[:, 0, :, lanes] = top.reshape(16, HALF, LANES)
            whole[:, 1, :, lanes] = bottom.reshape(16, HALF, LANES)
    lhs = left[...].reshape(512, 512)
    rhs = right[...].reshape(512, 512)
    if incoming:
        lhs = lhs.astype(F32).T.astype(BF16)
    dims = (((1,), (0 if incoming else 1,)), ((), ()))
    mixed = lax.dot_general(lhs, rhs, dims, preferred_element_type=F32).astype(BF16)
    mixed = mixed.reshape(16, 2, HALF, 512)
    for pair in range(4):
        lanes = slice(pair * LANES, (pair + 1) * LANES)
        top = mixed[:, 0, :, lanes].reshape(16 * HALF, LANES)
        bottom = mixed[:, 1, :, lanes].reshape(16 * HALF, LANES)
        a = jnp.concatenate([top[:, :COLS], bottom[:, :COLS]], axis=1)
        b = jnp.concatenate([top[:, COLS:], bottom[:, COLS:]], axis=1)
        for row in range(16):
            tile = slice(row * HALF, (row + 1) * HALF)
            out_ref[order.index(row * 8 + 2 * pair)] = a[tile]
            out_ref[order.index(row * 8 + 2 * pair + 1)] = b[tile]


def unpack(mixed_ref, rows):
    for h in range(DEVS):
        rows[h * ROW_STEP : h * ROW_STEP + HALF, :] = mixed_ref[h].astype(F32)


def scaled_step(rows, s):
    value = rows[pl.ds(s, DEVS, stride=ROW_STEP), :]
    center = value - jnp.mean(value, axis=0, keepdims=True)
    spread = jnp.mean(center * center, axis=0, keepdims=True)
    return (center * lax.rsqrt(jnp.maximum(spread, 1.0))).astype(BF16)


def finish(rows, s0, count, w_out, res_ref, gate_ref):
    lanes = slice(s0 * LANES, (s0 + count) * LANES)
    scaled = jnp.concatenate([scaled_step(rows, s0 + n) for n in range(count)], axis=1)
    update = jnp.dot(w_out, scaled, preferred_element_type=F32)
    return (res_ref[:, lanes].astype(F32) + gate_ref[:, lanes] * update).astype(BF16)


def middle_kernel(
    mixed_ref, mask_ref, res_ref, gate_ref, w_out_ref, w_in_ref,
    pieces_ref, first_ref, next_gate_ref, rows, stage,
):
    unpack(mixed_ref, rows)
    starts = range(0, HALF, 8)
    tiles = [finish(rows, s, 8, w_out_ref[...], res_ref, gate_ref) for s in starts]
    for s, x in zip(starts, tiles):
        lanes = slice(s * LANES, (s + 8) * LANES)
        first_ref[:, lanes] = x
        p = project(x.astype(F32), w_in_ref[...])
        stage_operands(p, mask_ref, stage, s)
        next_gate_ref[:, lanes] = sigmoid(p[512:])
    put_pieces(stage, pieces_ref)


def last_kernel(mixed_ref, res_ref, gate_ref, w_out_ref, up_ref, down_ref, out_ref, rows):
    unpack(mixed_ref, rows)
    starts = range(0, HALF, 8)
    tiles = [finish(rows, s, 8, w_out_ref[...], res_ref, gate_ref) for s in starts]
    for s, x in zip(starts, tiles):
        x = x.astype(F32)
        p = project(x, up_ref[...])
        half = (0.5 * p[:512]).astype(BF16)
        hidden = (half * jnp.tanh(half) + half) * p[512:].astype(BF16)
        y = x + jnp.dot(down_ref[...], hidden, preferred_element_type=F32)
        y = y.astype(BF16).T
        for n in range(8):
            out_ref[s + n] = y[2 * n * COLS : (2 * n + 1) * COLS]
            out_ref[HALF + s + n] = y[(2 * n + 1) * COLS : (2 * n + 2) * COLS]


VMEM = pl.BlockSpec(memory_space=pltpu.VMEM)
ANY = pl.BlockSpec(memory_space=pl.ANY)
PIECES = jax.ShapeDtypeStruct((DEVS, 2 * HALF, LANES), BF16)
MASK = jax.ShapeDtypeStruct((HALF, LANES), F32)
MIXED = jax.ShapeDtypeStruct((DEVS, HALF, LANES), BF16)
GATE = jax.ShapeDtypeStruct((CHANS, SPOTS), F32)
RES = jax.ShapeDtypeStruct((CHANS, SPOTS), BF16)
TILE = jax.ShapeDtypeStruct((ROWS, COLS, CHANS), BF16)
STAGE_T = pltpu.VMEM(((DEVS + 1) * STAGE, LANES), F32)
ROWS_T = pltpu.VMEM(((DEVS + 1) * ROW_STEP, LANES), F32)


def local(kernel, out, scratch, args, limit=32, flops=0, moved=0):
    return pl.pallas_call(
        kernel,
        out_shape=out,
        in_specs=[VMEM] * len(args),
        out_specs=jax.tree.map(lambda _: VMEM, out),
        scratch_shapes=scratch,
        compiler_params=pltpu.CompilerParams(vmem_limit_bytes=limit << 20),
        cost_estimate=pl.CostEstimate(flops=flops, bytes_accessed=moved, transcendentals=0),
    )(*args)


def first(residue_mask, pair, w_in):
    return pl.pallas_call(
        first_kernel,
        out_shape=(PIECES, MASK),
        in_specs=[ANY] * 3,
        out_specs=(VMEM, VMEM),
        scratch_shapes=[
            pltpu.VMEM((ROWS, COLS, CHANS), BF16),
            pltpu.VMEM((CHANS, 512), BF16),
            pltpu.VMEM((4, LANES), jnp.int32),
            STAGE_T,
            pltpu.SemaphoreType.DMA((3,)),
        ],
        compiler_params=pltpu.CompilerParams(vmem_limit_bytes=60 << 20),
    )(pair, w_in, residue_mask.reshape(4, LANES))


def weight(rows, cols=CHANS):
    return jax.ShapeDtypeStruct((rows, cols), BF16)


def side(*args):
    out = (GATE, RES, weight(128), weight(640), weight(128), weight(1024), weight(128, 512))
    channels = pltpu.VMEM((DEVS, CHANS), F32)
    return local(side_kernel, out, [channels, channels], args, flops=1 << 28, moved=6 << 20)


def product(incoming, order, pieces):
    whole = pltpu.VMEM((16, 2, HALF, 512), BF16)
    kernel = functools.partial(product_kernel, incoming, order)
    return local(kernel, MIXED, [whole, whole], (pieces.reshape(16, 8, 2 * HALF, LANES),))


def middle(*args):
    return local(middle_kernel, (PIECES, RES, GATE), [ROWS_T, STAGE_T], args)


def last(*args):
    return local(last_kernel, TILE, [ROWS_T], args)


def exchange(x, order=NATURAL):
    groups = None if order == NATURAL else [list(order)]
    return lax.all_to_all(x, ("row", "col"), 0, 0, axis_index_groups=groups, tiled=True)


def on_device(
    pair, residue_mask, out_in_w, out_gate_w, out_out_w, inc_in_w, inc_gate_w, inc_out_w,
    trans_up, trans_down,
):
    pieces, mask = first(residue_mask, pair, out_in_w)
    pair, pieces = lax.optimization_barrier((pair, pieces))
    beside = side(pair, out_gate_w, out_out_w, inc_in_w, inc_gate_w, inc_out_w, trans_up, trans_down)
    pieces, beside = lax.optimization_barrier((exchange(pieces), beside))
    gate, res, out_t, in_t, next_out_t, up_t, down_t = beside
    mixed = exchange(product(False, NATURAL, pieces))
    pieces, res, gate = middle(mixed, mask, res, gate, out_t, in_t)
    mixed = exchange(product(True, FAR_FIRST, exchange(pieces)), FAR_FIRST)
    return last(mixed, res, gate, next_out_t, up_t, down_t)


def solution(mesh):
    in_specs = (P("row", "col", None), P(), P(), P(), P(), P(), P(), P(), P(), P())
    out_specs = P("row", "col", None)
    return jax.shard_map(
        on_device, mesh=mesh, in_specs=in_specs, out_specs=out_specs, check_vma=False
    )
```

```python
import functools

import jax
import jax.numpy as jnp
from jax import lax
from jax.experimental import pallas as pl
from jax.experimental.pallas import tpu as pltpu
from jax.sharding import PartitionSpec as P

F32 = jnp.float32
BF16 = jnp.bfloat16
ROWS, COLS, CHANS = 32, 64, 128
HALF = ROWS // 2
LANES = 2 * COLS
SPOTS = ROWS * COLS
DEVS = 128
NATURAL = tuple(range(DEVS))


def far_first():
    def place(device):
        row, col = divmod(device, 8)
        at = (row // 4, col % 2 * 2 + row // 2 % 2, col // 2)
        return sum(min(k, 4 - k) for k in at), at, row % 2

    return tuple(sorted(range(DEVS), key=place, reverse=True))


FAR_FIRST = far_first()
STAGE = 40
ROW_STEP = 24


def normalize(x):
    center = x - jnp.mean(x, axis=0, keepdims=True)
    spread = jnp.mean(center * center, axis=0, keepdims=True)
    return (center * lax.rsqrt(spread + 1e-05)).astype(BF16)


def sigmoid(x):
    return 0.5 * jnp.tanh(0.5 * x) + 0.5


def put_mask(present_ref, mask_ref):
    row0 = lax.axis_index("row") * ROWS
    col = lax.axis_index("col")
    lane = lax.broadcasted_iota(jnp.int32, (HALF, LANES), 1)
    step = lax.broadcasted_iota(jnp.int32, (HALF, LANES), 0)
    low = lane < COLS
    line = present_ref[pl.ds(col // 2, 1), :].astype(F32)
    cols = jnp.where(low == ((col % 2) == 0), line, pltpu.roll(line, COLS, 1))
    line = present_ref[pl.ds(row0 // LANES, 1), :].astype(F32)
    spot = lane - row0 % LANES
    top = jnp.sum(jnp.where(spot == step, line, 0.0), axis=1, keepdims=True)
    bottom = jnp.sum(jnp.where(spot == step + HALF, line, 0.0), axis=1, keepdims=True)
    mask_ref[...] = cols * jnp.where(low, top, bottom)


def project(x, w):
    return jnp.dot(w, normalize(x), preferred_element_type=F32)


def stage_operands(p, mask_ref, stage):
    half_mask = 0.5 * jnp.concatenate([mask_ref[s : s + 1, :] for s in range(HALF)], axis=1)
    for at, k in ((0, 0), (HALF, 256)):
        value = half_mask * p[k + 128 : k + 256]
        value = value * jnp.tanh(0.5 * p[k : k + 128]) + value
        for s in range(HALF):
            stage[pl.ds(at + s, DEVS, stride=STAGE), :] = value[:, s * LANES : (s + 1) * LANES]


def put_pieces(stage, pieces_ref):
    for h in range(DEVS):
        pieces_ref[h] = stage[h * STAGE : h * STAGE + 2 * HALF, :].astype(BF16)


def load_steps(pair_ref, s0, count):
    blocks = []
    for s in range(s0, s0 + count):
        blocks += [pair_ref[s], pair_ref[HALF + s]]
    return jnp.concatenate(blocks, axis=0).T


def first_kernel(
    pair_hbm, w_in_hbm, present_hbm, pieces_ref, mask_ref, pair_ref, w_in_ref, present_ref, stage, sems
):
    moves = ((pair_hbm, pair_ref), (w_in_hbm, w_in_ref), (present_hbm, present_ref))
    copies = [pltpu.make_async_copy(a, b, sems.at[n]) for n, (a, b) in enumerate(moves)]
    for copy in copies:
        copy.start()
    for copy in copies:
        copy.wait()
    put_mask(present_ref, mask_ref)
    w = w_in_ref[...].T
    p = project(load_steps(pair_ref, 0, HALF).astype(F32), w)
    stage_operands(p, mask_ref, stage)
    put_pieces(stage, pieces_ref)


def side_kernel(
    pair_ref, gate_w_ref, out_w_ref, in_w_ref, next_gate_w_ref, next_out_w_ref, up_ref, down_ref,
    gate_ref, res_ref, out_t_ref, in_t_ref, next_out_t_ref, up_t_ref, down_t_ref, channels, ordered,
):
    w = gate_w_ref[...].T
    for s in range(0, HALF, 8):
        lanes = slice(s * LANES, (s + 8) * LANES)
        x = load_steps(pair_ref, s, 8)
        res_ref[:, lanes] = x
        gate_ref[:, lanes] = sigmoid(project(x.astype(F32), w))
    out_t_ref[...] = out_w_ref[...].T
    in_t_ref[:512] = in_w_ref[...].T
    in_t_ref[512:] = next_gate_w_ref[...].T
    channels[...] = next_out_w_ref[...].astype(F32)
    for n, channel in enumerate(FAR_FIRST):
        ordered[n : n + 1, :] = channels[channel : channel + 1, :]
    next_out_t_ref[...] = ordered[...].T.astype(BF16)
    up_t_ref[...] = up_ref[...].T
    down_t_ref[...] = down_ref[...].T


def product_kernel(incoming, order, x_ref, out_ref, left, right):
    for at, whole in ((0, left), (HALF, right)):
        for pair in range(4):
            a = x_ref[:, 2 * pair, at : at + HALF, :].reshape(16 * HALF, LANES)
            b = x_ref[:, 2 * pair + 1, at : at + HALF, :].reshape(16 * HALF, LANES)
            top = jnp.concatenate([a[:, :COLS], b[:, :COLS]], axis=1)
            bottom = jnp.concatenate([a[:, COLS:], b[:, COLS:]], axis=1)
            lanes = slice(pair * LANES, (pair + 1) * LANES)
            whole[:, 0, :, lanes] = top.reshape(16, HALF, LANES)
            whole[:, 1, :, lanes] = bottom.reshape(16, HALF, LANES)
    lhs = left[...].reshape(512, 512)
    rhs = right[...].reshape(512, 512)
    if incoming:
        lhs = lhs.astype(F32).T.astype(BF16)
    dims = (((1,), (0 if incoming else 1,)), ((), ()))
    mixed = lax.dot_general(lhs, rhs, dims, preferred_element_type=F32).astype(BF16)
    mixed = mixed.reshape(16, 2, HALF, 512)
    for pair in range(4):
        lanes = slice(pair * LANES, (pair + 1) * LANES)
        top = mixed[:, 0, :, lanes].reshape(16 * HALF, LANES)
        bottom = mixed[:, 1, :, lanes].reshape(16 * HALF, LANES)
        a = jnp.concatenate([top[:, :COLS], bottom[:, :COLS]], axis=1)
        b = jnp.concatenate([top[:, COLS:], bottom[:, COLS:]], axis=1)
        for row in range(16):
            tile = slice(row * HALF, (row + 1) * HALF)
            out_ref[order.index(row * 8 + 2 * pair)] = a[tile]
            out_ref[order.index(row * 8 + 2 * pair + 1)] = b[tile]


def unpack(mixed_ref, rows):
    for h in range(DEVS):
        rows[h * ROW_STEP : h * ROW_STEP + HALF, :] = mixed_ref[h].astype(F32)


def scaled_step(rows, s):
    value = rows[pl.ds(s, DEVS, stride=ROW_STEP), :]
    center = value - jnp.mean(value, axis=0, keepdims=True)
    spread = jnp.mean(center * center, axis=0, keepdims=True)
    return (center * lax.rsqrt(jnp.maximum(spread, 1.0))).astype(BF16)


def finish(rows, s0, count, w_out, res_ref, gate_ref):
    lanes = slice(s0 * LANES, (s0 + count) * LANES)
    scaled = jnp.concatenate([scaled_step(rows, s0 + n) for n in range(count)], axis=1)
    update = jnp.dot(w_out, scaled, preferred_element_type=F32)
    return (res_ref[:, lanes].astype(F32) + gate_ref[:, lanes] * update).astype(BF16)


def middle_kernel(
    mixed_ref, mask_ref, res_ref, gate_ref, w_out_ref, w_in_ref,
    pieces_ref, first_ref, next_gate_ref, rows, stage,
):
    unpack(mixed_ref, rows)
    x = finish(rows, 0, HALF, w_out_ref[...], res_ref, gate_ref)
    first_ref[...] = x
    p = project(x.astype(F32), w_in_ref[...])
    stage_operands(p, mask_ref, stage)
    next_gate_ref[...] = sigmoid(p[512:])
    put_pieces(stage, pieces_ref)


def last_kernel(mixed_ref, res_ref, gate_ref, w_out_ref, up_ref, down_ref, out_ref, rows):
    unpack(mixed_ref, rows)
    starts = range(0, HALF, 8)
    tiles = [finish(rows, s, 8, w_out_ref[...], res_ref, gate_ref) for s in starts]
    for s, x in zip(starts, tiles):
        x = x.astype(F32)
        p = project(x, up_ref[...])
        half = (0.5 * p[:512]).astype(BF16)
        hidden = (half * jnp.tanh(half) + half) * p[512:].astype(BF16)
        y = x + jnp.dot(down_ref[...], hidden, preferred_element_type=F32)
        y = y.astype(BF16).T
        for n in range(8):
            out_ref[s + n] = y[2 * n * COLS : (2 * n + 1) * COLS]
            out_ref[HALF + s + n] = y[(2 * n + 1) * COLS : (2 * n + 2) * COLS]


VMEM = pl.BlockSpec(memory_space=pltpu.VMEM)
ANY = pl.BlockSpec(memory_space=pl.ANY)
PIECES = jax.ShapeDtypeStruct((DEVS, 2 * HALF, LANES), BF16)
MASK = jax.ShapeDtypeStruct((HALF, LANES), F32)
MIXED = jax.ShapeDtypeStruct((DEVS, HALF, LANES), BF16)
GATE = jax.ShapeDtypeStruct((CHANS, SPOTS), F32)
RES = jax.ShapeDtypeStruct((CHANS, SPOTS), BF16)
TILE = jax.ShapeDtypeStruct((ROWS, COLS, CHANS), BF16)
STAGE_T = pltpu.VMEM(((DEVS + 1) * STAGE, LANES), F32)
ROWS_T = pltpu.VMEM(((DEVS + 1) * ROW_STEP, LANES), F32)


def local(kernel, out, scratch, args, limit=32, flops=0, moved=0):
    return pl.pallas_call(
        kernel,
        out_shape=out,
        in_specs=[VMEM] * len(args),
        out_specs=jax.tree.map(lambda _: VMEM, out),
        scratch_shapes=scratch,
        compiler_params=pltpu.CompilerParams(vmem_limit_bytes=limit << 20),
        cost_estimate=pl.CostEstimate(flops=flops, bytes_accessed=moved, transcendentals=0),
    )(*args)


def first(residue_mask, pair, w_in):
    return pl.pallas_call(
        first_kernel,
        out_shape=(PIECES, MASK),
        in_specs=[ANY] * 3,
        out_specs=(VMEM, VMEM),
        scratch_shapes=[
            pltpu.VMEM((ROWS, COLS, CHANS), BF16),
            pltpu.VMEM((CHANS, 512), BF16),
            pltpu.VMEM((4, LANES), jnp.int32),
            STAGE_T,
            pltpu.SemaphoreType.DMA((3,)),
        ],
        compiler_params=pltpu.CompilerParams(vmem_limit_bytes=60 << 20),
    )(pair, w_in, residue_mask.reshape(4, LANES))


def weight(rows, cols=CHANS):
    return jax.ShapeDtypeStruct((rows, cols), BF16)


def side(*args):
    out = (GATE, RES, weight(128), weight(640), weight(128), weight(1024), weight(128, 512))
    channels = pltpu.VMEM((DEVS, CHANS), F32)
    return local(side_kernel, out, [channels, channels], args, flops=1 << 28, moved=6 << 20)


def product(incoming, order, pieces):
    whole = pltpu.VMEM((16, 2, HALF, 512), BF16)
    kernel = functools.partial(product_kernel, incoming, order)
    return local(kernel, MIXED, [whole, whole], (pieces.reshape(16, 8, 2 * HALF, LANES),))


def middle(*args):
    return local(middle_kernel, (PIECES, RES, GATE), [ROWS_T, STAGE_T], args)


def last(*args):
    return local(last_kernel, TILE, [ROWS_T], args)


def exchange(x, order=NATURAL):
    groups = None if order == NATURAL else [list(order)]
    return lax.all_to_all(x, ("row", "col"), 0, 0, axis_index_groups=groups, tiled=True)


def on_device(
    pair, residue_mask, out_in_w, out_gate_w, out_out_w, inc_in_w, inc_gate_w, inc_out_w,
    trans_up, trans_down,
):
    pieces, mask = first(residue_mask, pair, out_in_w)
    pair, pieces = lax.optimization_barrier((pair, pieces))
    beside = side(pair, out_gate_w, out_out_w, inc_in_w, inc_gate_w, inc_out_w, trans_up, trans_down)
    pieces, beside = lax.optimization_barrier((exchange(pieces), beside))
    gate, res, out_t, in_t, next_out_t, up_t, down_t = beside
    mixed = exchange(product(False, NATURAL, pieces))
    pieces, res, gate = middle(mixed, mask, res, gate, out_t, in_t)
    mixed = exchange(product(True, FAR_FIRST, exchange(pieces)), FAR_FIRST)
    return last(mixed, res, gate, next_out_t, up_t, down_t)


def solution(mesh):
    in_specs = (P("row", "col", None), P(), P(), P(), P(), P(), P(), P(), P(), P())
    out_specs = P("row", "col", None)
    return jax.shard_map(
        on_device, mesh=mesh, in_specs=in_specs, out_specs=out_specs, check_vma=False
    )
```

```python
import functools

import jax
import jax.numpy as jnp
from jax import lax
from jax.experimental import pallas as pl
from jax.experimental.pallas import tpu as pltpu
from jax.sharding import PartitionSpec as P

F32 = jnp.float32
BF16 = jnp.bfloat16
ROWS, COLS, CHANS = 32, 64, 128
HALF = ROWS // 2
LANES = 2 * COLS
SPOTS = ROWS * COLS
DEVS = 128
NATURAL = tuple(range(DEVS))


def far_first():
    def place(device):
        row, col = divmod(device, 8)
        at = (row // 4, col % 2 * 2 + row // 2 % 2, col // 2)
        return sum(min(k, 4 - k) for k in at), at, row % 2

    return tuple(sorted(range(DEVS), key=place, reverse=True))


FAR_FIRST = far_first()
STAGE = 40
ROW_STEP = 24


def normalize(x):
    center = x - jnp.mean(x, axis=0, keepdims=True)
    spread = jnp.mean(center * center, axis=0, keepdims=True)
    return (center * lax.rsqrt(spread + 1e-05)).astype(BF16)


def sigmoid(x):
    return 0.5 * jnp.tanh(0.5 * x) + 0.5


def put_mask(present_ref, mask_ref):
    row0 = lax.axis_index("row") * ROWS
    col = lax.axis_index("col")
    lane = lax.broadcasted_iota(jnp.int32, (HALF, LANES), 1)
    step = lax.broadcasted_iota(jnp.int32, (HALF, LANES), 0)
    low = lane < COLS
    line = present_ref[pl.ds(col // 2, 1), :].astype(F32)
    cols = jnp.where(low == ((col % 2) == 0), line, pltpu.roll(line, COLS, 1))
    line = present_ref[pl.ds(row0 // LANES, 1), :].astype(F32)
    spot = lane - row0 % LANES
    top = jnp.sum(jnp.where(spot == step, line, 0.0), axis=1, keepdims=True)
    bottom = jnp.sum(jnp.where(spot == step + HALF, line, 0.0), axis=1, keepdims=True)
    mask_ref[...] = cols * jnp.where(low, top, bottom)


def project(x, w):
    return jnp.dot(w, normalize(x), preferred_element_type=F32)


def stage_operands(p, mask_ref, stage):
    half_mask = 0.5 * jnp.concatenate([mask_ref[s : s + 1, :] for s in range(HALF)], axis=1)
    for at, k in ((0, 0), (HALF, 256)):
        value = half_mask * p[k + 128 : k + 256]
        value = value * jnp.tanh(0.5 * p[k : k + 128]) + value
        for s in range(HALF):
            stage[pl.ds(at + s, DEVS, stride=STAGE), :] = value[:, s * LANES : (s + 1) * LANES]


def put_pieces(stage, pieces_ref):
    for h in range(DEVS):
        pieces_ref[h] = stage[h * STAGE : h * STAGE + 2 * HALF, :].astype(BF16)


def load_steps(pair_ref, s0, count):
    blocks = []
    for s in range(s0, s0 + count):
        blocks += [pair_ref[s], pair_ref[HALF + s]]
    return jnp.concatenate(blocks, axis=0).T


def first_kernel(
    pair_hbm, w_in_hbm, present_hbm, pieces_ref, mask_ref, pair_ref, w_in_ref, present_ref, stage, sems
):
    moves = ((pair_hbm, pair_ref), (w_in_hbm, w_in_ref), (present_hbm, present_ref))
    copies = [pltpu.make_async_copy(a, b, sems.at[n]) for n, (a, b) in enumerate(moves)]
    for copy in copies:
        copy.start()
    for copy in copies:
        copy.wait()
    put_mask(present_ref, mask_ref)
    w = w_in_ref[...].T
    p = project(load_steps(pair_ref, 0, HALF).astype(F32), w)
    stage_operands(p, mask_ref, stage)
    put_pieces(stage, pieces_ref)


def side_kernel(
    pair_ref, gate_w_ref, out_w_ref, in_w_ref, next_gate_w_ref, next_out_w_ref, up_ref, down_ref,
    gate_ref, res_ref, out_t_ref, in_t_ref, next_out_t_ref, up_t_ref, down_t_ref, channels, ordered,
):
    w = gate_w_ref[...].T
    for s in range(0, HALF, 8):
        lanes = slice(s * LANES, (s + 8) * LANES)
        x = load_steps(pair_ref, s, 8)
        res_ref[:, lanes] = x
        gate_ref[:, lanes] = sigmoid(project(x.astype(F32), w)).astype(BF16)
    out_t_ref[...] = out_w_ref[...].T
    in_t_ref[:512] = in_w_ref[...].T
    in_t_ref[512:] = next_gate_w_ref[...].T
    channels[...] = next_out_w_ref[...].astype(F32)
    for n, channel in enumerate(FAR_FIRST):
        ordered[n : n + 1, :] = channels[channel : channel + 1, :]
    next_out_t_ref[...] = ordered[...].T.astype(BF16)
    up_t_ref[...] = up_ref[...].T
    down_t_ref[...] = down_ref[...].T


def product_kernel(incoming, order, x_ref, out_ref, left, right):
    for at, whole in ((0, left), (HALF, right)):
        for pair in range(4):
            a = x_ref[:, 2 * pair, at : at + HALF, :].reshape(16 * HALF, LANES)
            b = x_ref[:, 2 * pair + 1, at : at + HALF, :].reshape(16 * HALF, LANES)
            top = jnp.concatenate([a[:, :COLS], b[:, :COLS]], axis=1)
            bottom = jnp.concatenate([a[:, COLS:], b[:, COLS:]], axis=1)
            lanes = slice(pair * LANES, (pair + 1) * LANES)
            whole[:, 0, :, lanes] = top.reshape(16, HALF, LANES)
            whole[:, 1, :, lanes] = bottom.reshape(16, HALF, LANES)
    lhs = left[...].reshape(512, 512)
    rhs = right[...].reshape(512, 512)
    if incoming:
        lhs = lhs.astype(F32).T.astype(BF16)
    dims = (((1,), (0 if incoming else 1,)), ((), ()))
    mixed = lax.dot_general(lhs, rhs, dims, preferred_element_type=F32).astype(BF16)
    mixed = mixed.reshape(16, 2, HALF, 512)
    for pair in range(4):
        lanes = slice(pair * LANES, (pair + 1) * LANES)
        top = mixed[:, 0, :, lanes].reshape(16 * HALF, LANES)
        bottom = mixed[:, 1, :, lanes].reshape(16 * HALF, LANES)
        a = jnp.concatenate([top[:, :COLS], bottom[:, :COLS]], axis=1)
        b = jnp.concatenate([top[:, COLS:], bottom[:, COLS:]], axis=1)
        for row in range(16):
            tile = slice(row * HALF, (row + 1) * HALF)
            out_ref[order.index(row * 8 + 2 * pair)] = a[tile]
            out_ref[order.index(row * 8 + 2 * pair + 1)] = b[tile]


def unpack(mixed_ref, rows):
    for h in range(DEVS):
        rows[h * ROW_STEP : h * ROW_STEP + HALF, :] = mixed_ref[h].astype(F32)


def scaled_step(rows, s):
    value = rows[pl.ds(s, DEVS, stride=ROW_STEP), :]
    center = value - jnp.mean(value, axis=0, keepdims=True)
    spread = jnp.mean(center * center, axis=0, keepdims=True)
    return (center * lax.rsqrt(jnp.maximum(spread, 1.0))).astype(BF16)


def finish(rows, s0, count, w_out, res_ref, gate_ref):
    lanes = slice(s0 * LANES, (s0 + count) * LANES)
    scaled = jnp.concatenate([scaled_step(rows, s0 + n) for n in range(count)], axis=1)
    update = jnp.dot(w_out, scaled, preferred_element_type=F32)
    return (res_ref[:, lanes].astype(F32) + gate_ref[:, lanes].astype(F32) * update).astype(BF16)


def middle_kernel(
    mixed_ref, mask_ref, res_ref, gate_ref, w_out_ref, w_in_ref,
    pieces_ref, first_ref, next_gate_ref, rows, stage,
):
    unpack(mixed_ref, rows)
    x = finish(rows, 0, HALF, w_out_ref[...], res_ref, gate_ref)
    first_ref[...] = x
    p = project(x.astype(F32), w_in_ref[...])
    stage_operands(p, mask_ref, stage)
    next_gate_ref[...] = sigmoid(p[512:]).astype(BF16)
    put_pieces(stage, pieces_ref)


def last_kernel(mixed_ref, res_ref, gate_ref, w_out_ref, up_ref, down_ref, out_ref, rows):
    unpack(mixed_ref, rows)
    starts = range(0, HALF, 8)
    tiles = [finish(rows, s, 8, w_out_ref[...], res_ref, gate_ref) for s in starts]
    for s, x in zip(starts, tiles):
        x = x.astype(F32)
        p = project(x, up_ref[...])
        half = (0.5 * p[:512]).astype(BF16)
        hidden = (half * jnp.tanh(half) + half) * p[512:].astype(BF16)
        y = x + jnp.dot(down_ref[...], hidden, preferred_element_type=F32)
        y = y.astype(BF16).T
        for n in range(8):
            out_ref[s + n] = y[2 * n * COLS : (2 * n + 1) * COLS]
            out_ref[HALF + s + n] = y[(2 * n + 1) * COLS : (2 * n + 2) * COLS]


VMEM = pl.BlockSpec(memory_space=pltpu.VMEM)
ANY = pl.BlockSpec(memory_space=pl.ANY)
PIECES = jax.ShapeDtypeStruct((DEVS, 2 * HALF, LANES), BF16)
MASK = jax.ShapeDtypeStruct((HALF, LANES), F32)
MIXED = jax.ShapeDtypeStruct((DEVS, HALF, LANES), BF16)
GATE = jax.ShapeDtypeStruct((CHANS, SPOTS), BF16)
RES = jax.ShapeDtypeStruct((CHANS, SPOTS), BF16)
TILE = jax.ShapeDtypeStruct((ROWS, COLS, CHANS), BF16)
STAGE_T = pltpu.VMEM(((DEVS + 1) * STAGE, LANES), F32)
ROWS_T = pltpu.VMEM(((DEVS + 1) * ROW_STEP, LANES), F32)


def local(kernel, out, scratch, args, limit=32, flops=0, moved=0):
    return pl.pallas_call(
        kernel,
        out_shape=out,
        in_specs=[VMEM] * len(args),
        out_specs=jax.tree.map(lambda _: VMEM, out),
        scratch_shapes=scratch,
        compiler_params=pltpu.CompilerParams(vmem_limit_bytes=limit << 20),
        cost_estimate=pl.CostEstimate(flops=flops, bytes_accessed=moved, transcendentals=0),
    )(*args)


def first(residue_mask, pair, w_in):
    return pl.pallas_call(
        first_kernel,
        out_shape=(PIECES, MASK),
        in_specs=[ANY] * 3,
        out_specs=(VMEM, VMEM),
        scratch_shapes=[
            pltpu.VMEM((ROWS, COLS, CHANS), BF16),
            pltpu.VMEM((CHANS, 512), BF16),
            pltpu.VMEM((4, LANES), jnp.int32),
            STAGE_T,
            pltpu.SemaphoreType.DMA((3,)),
        ],
        compiler_params=pltpu.CompilerParams(vmem_limit_bytes=60 << 20),
    )(pair, w_in, residue_mask.reshape(4, LANES))


def weight(rows, cols=CHANS):
    return jax.ShapeDtypeStruct((rows, cols), BF16)


def side(*args):
    out = (GATE, RES, weight(128), weight(640), weight(128), weight(1024), weight(128, 512))
    channels = pltpu.VMEM((DEVS, CHANS), F32)
    return local(side_kernel, out, [channels, channels], args, flops=1 << 28, moved=6 << 20)


def product(incoming, order, pieces):
    whole = pltpu.VMEM((16, 2, HALF, 512), BF16)
    kernel = functools.partial(product_kernel, incoming, order)
    return local(kernel, MIXED, [whole, whole], (pieces.reshape(16, 8, 2 * HALF, LANES),))


def middle(*args):
    return local(middle_kernel, (PIECES, RES, GATE), [ROWS_T, STAGE_T], args)


def last(*args):
    return local(last_kernel, TILE, [ROWS_T], args)


def exchange(x, order=NATURAL):
    groups = None if order == NATURAL else [list(order)]
    return lax.all_to_all(x, ("row", "col"), 0, 0, axis_index_groups=groups, tiled=True)


def on_device(
    pair, residue_mask, out_in_w, out_gate_w, out_out_w, inc_in_w, inc_gate_w, inc_out_w,
    trans_up, trans_down,
):
    pieces, mask = first(residue_mask, pair, out_in_w)
    pair, pieces = lax.optimization_barrier((pair, pieces))
    beside = side(pair, out_gate_w, out_out_w, inc_in_w, inc_gate_w, inc_out_w, trans_up, trans_down)
    pieces, beside = lax.optimization_barrier((exchange(pieces), beside))
    gate, res, out_t, in_t, next_out_t, up_t, down_t = beside
    mixed = exchange(product(False, NATURAL, pieces))
    pieces, res, gate = middle(mixed, mask, res, gate, out_t, in_t)
    mixed = exchange(product(True, FAR_FIRST, exchange(pieces)), FAR_FIRST)
    return last(mixed, res, gate, next_out_t, up_t, down_t)


def solution(mesh):
    in_specs = (P("row", "col", None), P(), P(), P(), P(), P(), P(), P(), P(), P())
    out_specs = P("row", "col", None)
    return jax.shard_map(
        on_device, mesh=mesh, in_specs=in_specs, out_specs=out_specs, check_vma=False
    )
```
